256 devices in a mesh: queue: 64 (over z, x, y_hi), shard: 4 (over y_lo, core).
Axes of the slice: x: 4, y: 4 (y_hi: 2, y_lo: 2; y = y_hi * 2 + y_lo), z: 8, core: 2. Of those that a mesh axis runs over, the one named last changes fastest.
Arguments:
- state: float32 [24576, 2560], P(('queue', 'shard')), may hold values from -150 to 150
- noise: bfloat16 [384, 2560], P('shard'), may hold values from -6 to 6
- modulation: bfloat16 [10, 3, 2560], replicated, may hold values from -3 to 3
- timesteps: int32 [64], P('queue'), may hold values from 0 to 9
- plan: float32 [11], replicated, may hold values from 0.02 to 1
- frame_ids: int32 [24576], replicated, may hold values from 0 to 511, never falling along the last dimension, each value on 1 to 96 neighbouring positions
- w_query: bfloat16 [2560, 2048], P(None, 'shard'), may hold values from -1 to 1
- w_key: bfloat16 [2560, 2048], P(None, 'shard'), may hold values from -40 to 40
- w_value: bfloat16 [2560, 2048], P(None, 'shard'), may hold values from -0.125 to 0.125
- w_out: bfloat16 [2048, 2560], P('shard'), may hold values from -0.125 to 0.125
Outputs:
- advanced: float32 [24576, 2560], P(('queue', 'shard'))
- estimate: bfloat16 [24576, 2560], P(('queue', 'shard'))
The draws below stay inside these ranges and needn't reach their ends.
Inputs may be any that keep to these rules, and one draw needn't show every extreme that they name: `frame_ids`: frame numbers never fall along the tokens; each frame covers 1 to 96 consecutive tokens, and one frame exactly 96.
All inputs are finite; a program needn't handle non-finite values.
Results may differ from the reference program's by a relative error of at most 0.007.
Values may be sent and summed in bfloat16 or wider, within the bound.
A program may use at most 64 MiB of HBM per device.

```python
import math
import jax
import jax.numpy as jnp
import numpy as np
from jax import lax

D = 2560
HEADS = 32
HEAD_DIM = 64
LEVELS = 10
TOK_DEV = 96
TOK_SLOT = 384
TOKENS = 24576
FRAME_MOST = 96
FRAMES = 512
N_QUEUE = 64
N_SHARD = 4


def common_projection(key):
    return jax.random.normal(key, (D, HEADS * HEAD_DIM), jnp.float32) / math.sqrt(D)


def draw_w_query(key, part):
    shared_part = common_projection(key)
    key = jax.random.fold_in(key, 5)
    jitter = jax.random.uniform(key, shared_part.shape, jnp.float32, 0.9, 1.1)
    return jnp.clip(shared_part * jitter, -1.0, 1.0).astype(jnp.bfloat16)


def draw_w_key(key, part):
    key = jax.random.fold_in(key, 6)
    own_key = jax.random.fold_in(key, 0)
    own_part = jax.random.normal(own_key, (D, HEADS * HEAD_DIM), jnp.float32) / math.sqrt(D)
    mixed = own_part
    return jnp.clip(mixed, -40.0, 40.0).astype(jnp.bfloat16)


def draw_state(key, part):
    key = jax.random.fold_in(key, 7)
    drawn_key = jax.random.fold_in(key, 0)
    drawn = jax.random.normal(drawn_key, (TOKENS, D), jnp.float32)
    return jnp.clip(drawn, -6.0, 6.0)


def touch_ends(result, key, least, largest):
    longest = result.shape.index(max(result.shape))
    spots = []
    for shift in (0, 1):
        where = [jax.random.randint(jax.random.fold_in(key, axis), (), 0, length) for axis, length in enumerate(result.shape)]
        where[longest] = (where[longest] + shift) % result.shape[longest]
        spots.append(tuple(where))
    return result.at[spots[0]].set(least).at[spots[1]].set(largest)


def shard_levels(stream_key, shape, pieces, smallest, largest):
    gain, own = 1.0, jax.random.fold_in(stream_key, 6)
    for axis_at, parts in pieces:
        heights = jnp.exp(jax.random.uniform(jax.random.fold_in(own, axis_at), (parts,), jnp.float32, smallest / len(pieces), largest / len(pieces)))
        gain = gain * jnp.repeat(heights, shape[axis_at] // parts).reshape([-1 if axis == axis_at else 1 for axis in range(len(shape))])
    return gain


def length_profile(number_of, total, reach, lean):
    loads = [(1 << 20) // math.isqrt(standing ** lean) + 1 for standing in range(2, number_of + 1)]
    surplus, given = total - reach - (number_of - 1), [1] * (number_of - 1)
    while surplus > 0:
        candidates = [i for i in range(number_of - 1) if given[i] < reach]
        whole, remaining = sum([loads[i] for i in candidates]), surplus
        for i in candidates:
            addition = min(reach - given[i], max(1, remaining * loads[i] // whole), surplus)
            given[i] = given[i] + addition
            surplus = surplus - addition
    return np.array([reach] + given)


def uneven_parts(key, count, total, most, slope):
    if count == 2:
        one = jax.random.randint(key, (), max(1, total - most), min(most, total - 1) + 1)
        return jnp.stack([one, total - one])
    sizes = jnp.asarray(length_profile(count, total, most, slope), jnp.int32)
    couples = (count - 1) // 2
    giver, sink = sizes[1:1 + 2 * couples:2], sizes[2:2 + 2 * couples:2]
    margin = jnp.minimum(giver - 1, most - sink)
    passed = jax.random.randint(jax.random.fold_in(key, 1), (couples,), 0, 1 << 20) % (margin + 1)
    sizes = sizes.at[1:1 + 2 * couples:2].set(giver - passed).at[2:2 + 2 * couples:2].set(sink + passed)
    return sizes[jax.random.permutation(jax.random.fold_in(key, 2), count)]


def bell_draw(rng, shape, scale, limit, shards=(), kind=jnp.bfloat16):
    values = jax.random.normal(rng, shape, jnp.float32) * scale
    if len(shards) > 0:
        values = shard_levels(rng, shape, shards, -0.22, 0.18) * values
    return jnp.clip(values, min=-limit, max=limit).astype(kind)


def setup_inputs(seed: int = 0) -> dict:
    streams_of = jax.random.split(jax.random.key(seed), 11)
    state = draw_state(jax.random.fold_in(streams_of[10], 71), 0)
    noise = bell_draw(streams_of[1], (TOK_SLOT, D), 1.0, 6.0, ((0, 4),))
    modulation = bell_draw(streams_of[2], (LEVELS, 3, D), 0.5, 3.0)
    timesteps = touch_ends(jax.random.randint(streams_of[3], (N_QUEUE,), 0, LEVELS), jax.random.fold_in(streams_of[3], 1), 0, LEVELS - 1).astype(jnp.int32)
    plan = jnp.clip(jnp.exp(jax.random.uniform(streams_of[4], (LEVELS + 1,), jnp.float32, math.log(0.02), math.log(1.0))), 0.02, 1.0)
    frame_ids = jnp.searchsorted(jnp.cumsum(uneven_parts(streams_of[5], FRAMES, TOKENS, FRAME_MOST, 0)), jnp.arange(TOKENS), side="right").astype(jnp.int32)
    w_query = draw_w_query(jax.random.fold_in(streams_of[10], 71), 0)
    w_key = draw_w_key(jax.random.fold_in(streams_of[10], 71), 0)
    w_value = bell_draw(streams_of[8], (D, HEADS * HEAD_DIM), D ** -0.5, 0.125, ((1, 4),))
    w_out = bell_draw(streams_of[9], (HEADS * HEAD_DIM, D), (HEADS * HEAD_DIM) ** -0.5, 0.125, ((0, 4),))
    return dict(state=state, noise=noise, modulation=modulation, timesteps=timesteps, plan=plan, frame_ids=frame_ids, w_query=w_query, w_key=w_key, w_value=w_value, w_out=w_out)


def normalize(hidden, modulate):
    center = lax.optimization_barrier(jnp.mean(hidden, axis=-1, keepdims=True))
    spread = lax.optimization_barrier(jnp.mean(jnp.square(hidden - center), axis=-1, keepdims=True))
    normed = (hidden - center) * lax.rsqrt(spread + 1e-06)
    return (normed * (1.0 + modulate[1]) + modulate[0]).astype(jnp.bfloat16)

def reference(state, noise, modulation, timesteps, plan, frame_ids, w_query, w_key, w_value, w_out):
    tok_slot = TOK_DEV * N_SHARD
    inner = HEADS * HEAD_DIM
    slots = state.reshape(N_QUEUE, tok_slot, D)

    def project(slot_index):
        hidden = slots[slot_index]
        modulate = modulation[timesteps[slot_index]].astype(jnp.float32)
        normed = normalize(hidden, modulate)
        return jnp.stack([jnp.dot(normed, weight, preferred_element_type=jnp.float32).astype(jnp.bfloat16) for weight in (w_query, w_key, w_value)])
    projected = lax.map(project, jnp.arange(N_QUEUE, dtype=jnp.int32))
    zero_slot = jnp.zeros((1, 2, tok_slot, inner), jnp.bfloat16)
    padded = jnp.concatenate([zero_slot, projected[:, 1:], zero_slot], axis=0)
    frames = jnp.pad(frame_ids, (tok_slot, tok_slot), constant_values=-(1 << 20)).reshape(N_QUEUE + 2, tok_slot)
    query_frames_all = frame_ids.reshape(N_QUEUE, tok_slot)
    head_group = inner // N_SHARD
    out_groups = w_out.astype(jnp.float32).reshape(N_SHARD, head_group, D)
    score_scale = 1.0 / math.sqrt(HEAD_DIM)

    def advance(slot_index):
        queries = projected[slot_index, 0].astype(jnp.float32).reshape(tok_slot, HEADS, HEAD_DIM)
        beside_all = lax.dynamic_slice_in_dim(padded, slot_index, 3, 0)
        key_heads = jnp.transpose(beside_all[:, 0], (0, 1, 2)).reshape(3 * tok_slot, HEADS, HEAD_DIM).astype(jnp.float32)
        value_heads = beside_all[:, 1].reshape(3 * tok_slot, HEADS, HEAD_DIM).astype(jnp.float32)
        key_frames = lax.dynamic_slice_in_dim(frames, slot_index, 3, 0).reshape(3 * tok_slot)
        query_frames = query_frames_all[slot_index]
        scores = jnp.einsum('qhd,khd->hqk', queries, key_heads) * score_scale
        allowed = jnp.abs(query_frames[:, None] - key_frames[None, :]) <= 1
        scores = jnp.where(allowed[None], scores, -1e+30)
        row_max = lax.optimization_barrier(jnp.max(scores, axis=-1, keepdims=True))
        weights = jnp.exp(scores - row_max)
        weights = (weights / lax.optimization_barrier(jnp.sum(weights, axis=-1, keepdims=True))).astype(jnp.bfloat16)
        mixed = jnp.einsum('hqk,khd->qhd', weights.astype(jnp.float32), value_heads).astype(jnp.bfloat16)
        grouped = mixed.reshape(tok_slot, N_SHARD, head_group).astype(jnp.float32)
        partials = jnp.einsum('qgi,gid->gqd', grouped, out_groups)
        attn_sum = lax.optimization_barrier(jnp.sum(partials.astype(jnp.bfloat16).astype(jnp.float32), axis=0))
        noise_level = timesteps[slot_index]
        modulate = modulation[noise_level].astype(jnp.float32)
        velocity = modulate[2] * attn_sum
        sigma_now = plan[noise_level]
        sigma_next = plan[noise_level + 1]
        hidden = slots[slot_index]
        estimate = (hidden - sigma_now * velocity).astype(jnp.bfloat16)
        moved = hidden + (sigma_next - sigma_now) * velocity
        return (moved, estimate)
    moved, estimate = lax.map(advance, jnp.arange(N_QUEUE, dtype=jnp.int32))
    advanced = jnp.concatenate([noise.astype(jnp.float32)[None], moved[:-1]], axis=0)
    return (advanced.reshape(N_QUEUE * tok_slot, D), estimate.reshape(N_QUEUE * tok_slot, D))
```

```python
import functools

import jax
import jax.numpy as jnp
from jax import lax
from jax.experimental import pallas as pl
from jax.experimental.pallas import tpu as pltpu
from jax.sharding import PartitionSpec as P

MESH = pl.DeviceIdType.MESH
ROWS = 96
HALF = 48
BF16 = jnp.bfloat16
F32 = jnp.float32


def kernel(
    state_h, noise_h, mod_ref, step_ref, plan_ref, frame_ref, wq_h, wk_h, wv_h, wo_h,
    adv_h, est_h,
    state, noise, blocks, w_in, w_out, queries, kv, bias, mixed, mixed_sib,
    own_sum, far_sum, far_in, moved, moved_in, adv, est,
    load_sem, store_sem, send_sem, recv_sem, pair_send, pair_recv,
    far_send, far_recv, move_send, move_recv,
):
    width = state.shape[1]
    inner = queries.shape[1]
    chunks, _, span = own_sum.shape
    pairs = inner // 128
    slots = lax.axis_size("queue")
    slot = lax.axis_index("queue")
    shard = lax.axis_index("shard")
    side = lax.div(shard, 2)
    core = lax.rem(shard, 2)
    other = 1 - core
    chain = 2 * slots
    chip = 2 * slot + side

    def at(step, which):
        there = lax.rem(chip + step + chain, chain)
        return (lax.div(there, 2), 2 * lax.rem(there, 2) + which)

    sibling = (slot, 2 * side + other)
    ahead = at(1, core)
    behind = at(-1, core)
    across = at(2 * core - 1, other)

    barrier = pltpu.get_barrier_semaphore()
    for device in (sibling, ahead, behind, across, at(-2, core)):
        pl.semaphore_signal(barrier, inc=1, device_id=device, device_id_type=MESH)

    def load(source, target, n):
        copy = pltpu.make_async_copy(source, target, load_sem.at[n])
        copy.start()
        return copy

    load_state = load(state_h, state, 0)
    load_w = [
        load(w, w_in.at[:, pl.ds(n * inner, inner)], 1 + n)
        for n, w in enumerate((wq_h, wk_h, wv_h))
    ]
    load_wo = load(wo_h, w_out.at[0], 4)
    load_noise = load(noise_h, noise, 5)

    level = step_ref[0]
    modulate = mod_ref[level].astype(F32)
    shift, gain, gate = modulate[0:1], 1.0 + modulate[1:2], modulate[2:3]
    sigma_now = plan_ref[level]
    sigma_step = plan_ref[level + 1] - sigma_now
    mine = blocks.at[4 + core]
    load_state.wait()

    def normalise(n, _):
        rows = pl.ds(pl.multiple_of(n * 16, 16), 16)
        x = state[rows, :]
        x = x - jnp.mean(x, axis=-1, keepdims=True)
        spread = jnp.mean(jnp.square(x), axis=-1, keepdims=True)
        blocks[4 + core, rows, :] = (x * lax.rsqrt(spread + 1e-06) * gain + shift).astype(BF16)
        return 0

    lax.fori_loop(0, ROWS // 16, normalise, 0)
    pl.semaphore_wait(barrier, 5)

    sends = []

    def send(place, half, to_place, device, n):
        rows = pl.ds(half * HALF, HALF)
        copy = pltpu.make_async_remote_copy(
            src_ref=blocks.at[place, rows],
            dst_ref=blocks.at[to_place, rows],
            send_sem=send_sem.at[n],
            recv_sem=recv_sem.at[to_place, half],
            device_id=device,
            device_id_type=MESH,
        )
        return copy

    def wait_block(place, half):
        rows = pl.ds(half * HALF, HALF)
        here = blocks.at[place, rows]
        pltpu.make_async_copy(here, here, recv_sem.at[place, half]).wait()

    for half in range(2):
        sends.append(send(4 + core, half, 2 + core, ahead, 3 * half))
        sends.append(send(4 + core, half, 6 + core, behind, 3 * half + 1))
        sends.append(send(4 + core, half, 4 + core, sibling, 3 * half + 2))
    for copy in sends:
        copy.start()
    share_w = pltpu.make_async_remote_copy(
        src_ref=wo_h, dst_ref=w_out.at[1], send_sem=pair_send.at[0], recv_sem=pair_recv.at[0],
        device_id=sibling, device_id_type=MESH,
    )
    share_w.start()

    first = 192 * chip - 288 + chain * 192
    row = lax.div(first, 128)
    lines = [
        frame_ref[pl.ds(lax.rem(row + n, chain * 192 // 128), 1), :] for n in range(7)
    ]
    line = jnp.concatenate(lines, axis=1).astype(F32)
    line = jnp.broadcast_to(line, (8, 896))
    line = jnp.where(side == 0, pltpu.roll(line, 896 - 96, 1), pltpu.roll(line, 896 - 32, 1))
    column = jnp.broadcast_to(pltpu.roll(line, 896 - 192, 1)[0:1, :384], (128, 384)).T
    for n in range(4):
        keys = line if n == 0 else pltpu.roll(line, 896 - 96 * n, 1)
        gap = jnp.abs(column[n * ROWS:(n + 1) * ROWS, 0:1] - keys[0:1, :512])
        bias[n] = jnp.where(gap <= 1.0, 0.0, -1e30)
    kv[pl.ds(8 * ROWS, 32), :] = jnp.zeros((32, 2 * inner), BF16)

    def project(place, count, col, target, target_row):
        def part(n, _):
            into = pl.multiple_of(n * 256, 256)
            x = blocks[pl.ds(place, count)].reshape(count * ROWS, width)
            y = jnp.dot(x, w_in[:, pl.ds(col + into, 256)], preferred_element_type=F32)
            target[pl.ds(target_row, count * ROWS), pl.ds(into, 256)] = y.astype(BF16)
            return 0
        return part

    def project_q(place, count, row_):
        def part(n, _):
            into = pl.multiple_of(n * 256, 256)
            x = blocks[place:place + count].reshape(count * ROWS, width)
            y = jnp.dot(x, w_in[:, pl.ds(into, 256)], preferred_element_type=F32)
            queries[pl.ds(row_, count * ROWS), pl.ds(into, 256)] = y.astype(BF16) * 0.125
            return 0
        lax.fori_loop(0, inner // 256, part, 0)

    def project_kv(place, rows_):
        def part(n, _):
            into = pl.multiple_of(n * 256, 256)
            x = blocks[place:place + 2].reshape(2 * ROWS, width)
            w = w_in[:, pl.ds(pl.multiple_of(inner + into, 256), 256)]
            y = jnp.dot(x, w, preferred_element_type=F32).astype(BF16)
            for k, row_ in enumerate(rows_):
                kv[pl.ds(row_, ROWS), pl.ds(into, 256)] = y[k * ROWS:(k + 1) * ROWS]
            return 0
        lax.fori_loop(0, 2 * inner // 256, part, 0)

    def attend(n):
        lane = lax.broadcasted_iota(jnp.int32, (ROWS, 128), 1)
        low = lane < 64

        def pair(g, _):
            cols = pl.ds(pl.multiple_of(g * 128, 128), 128)
            v_cols = pl.ds(pl.multiple_of(inner + g * 128, 128), 128)
            q = queries[pl.ds(n * ROWS, ROWS), cols]
            zero = jnp.zeros_like(q)
            q = jnp.concatenate([jnp.where(low, q, zero), jnp.where(low, zero, q)], axis=0)
            k = kv[pl.ds(n * ROWS, 512), cols]
            v = kv[pl.ds(n * ROWS, 512), v_cols]
            s = lax.dot_general(q, k, (((1,), (1,)), ((), ())), preferred_element_type=F32)
            s = s + jnp.concatenate([bias[n], bias[n]], axis=0)
            w = jnp.exp(s - jnp.max(s, axis=-1, keepdims=True))
            total = jnp.sum(w, axis=-1, keepdims=True)
            o = jnp.dot(w.astype(BF16), v, preferred_element_type=F32) / total
            mixed[n, :, cols] = jnp.where(low, o[:ROWS], o[ROWS:]).astype(BF16)
            return 0
        lax.fori_loop(0, pairs, pair, 0)

    for half in range(2):
        wait_block(4 + other, half)
    for copy in load_w:
        copy.wait()
    project_q(4, 2, ROWS)
    project_kv(4, (3 * ROWS, 4 * ROWS))

    def forward(place, half, n):
        wait_block(place, half)
        send(place, half, place, sibling, n).start()

    def relay_ahead():
        rows = pl.ds(pl.multiple_of(core * HALF, 16), HALF)
        return pltpu.make_async_remote_copy(
            src_ref=blocks.at[3, rows], dst_ref=blocks.at[1, rows],
            send_sem=send_sem.at[10], recv_sem=recv_sem.at[1, core],
            device_id=ahead, device_id_type=MESH,
        )

    def relay_behind():
        rows = pl.ds(pl.multiple_of(core * HALF, 16), HALF)
        return pltpu.make_async_remote_copy(
            src_ref=blocks.at[6, rows], dst_ref=blocks.at[0, rows],
            send_sem=send_sem.at[11], recv_sem=recv_sem.at[0, core],
            device_id=behind, device_id_type=MESH,
        )

    @pl.when(core == 0)
    def _():
        forward(2, 0, 6)
        forward(6, 0, 7)
        relay_behind().start()
        wait_block(3, 0)
        relay_ahead().start()
        forward(2, 1, 8)
        forward(6, 1, 9)
        wait_block(3, 1)
        wait_block(7, 0)
        wait_block(7, 1)

    @pl.when(core == 1)
    def _():
        forward(3, 0, 6)
        forward(7, 0, 7)
        forward(3, 1, 8)
        relay_ahead().start()
        forward(7, 1, 9)
        wait_block(6, 0)
        wait_block(6, 1)
        relay_behind().start()
        wait_block(2, 0)
        wait_block(2, 1)

    project_q(3, 1, 0)
    project_q(6, 1, 3 * ROWS)
    project_kv(2, (ROWS, 2 * ROWS))
    project_kv(6, (5 * ROWS, 6 * ROWS))
    attend(1)
    attend(2)

    for k in range(2):
        rows = pl.ds(pl.multiple_of(core * HALF, 16), HALF)
        here = blocks.at[k, rows]
        pltpu.make_async_copy(here, here, recv_sem.at[k, core]).wait()
        pltpu.make_async_remote_copy(
            src_ref=here, dst_ref=here, send_sem=send_sem.at[12 + k],
            recv_sem=recv_sem.at[k, core], device_id=sibling, device_id_type=MESH,
        ).start()
    for k in range(2):
        rows = pl.ds(pl.multiple_of(other * HALF, 16), HALF)
        here = blocks.at[k, rows]
        pltpu.make_async_copy(here, here, recv_sem.at[k, other]).wait()
    project_kv(0, (7 * ROWS, 0))
    attend(0)
    attend(3)

    theirs = pl.ds(pl.multiple_of(other * HALF, 16), HALF)
    ours = pl.ds(pl.multiple_of(core * HALF, 16), HALF)
    swaps = []
    for n, (source, start, count) in enumerate((
        (mixed.at[0, theirs], 0, HALF),
        (mixed.at[3, theirs], HALF, HALF),
        (mixed.at[1 + other], ROWS, ROWS),
    )):
        swaps.append(pltpu.make_async_remote_copy(
            src_ref=source, dst_ref=mixed_sib.at[pl.ds(start, count)],
            send_sem=pair_send.at[1 + n], recv_sem=pair_recv.at[1 + n],
            device_id=sibling, device_id_type=MESH,
        ))
    for copy in swaps:
        copy.start()
    load_wo.wait()
    share_w.wait()
    for copy in swaps:
        copy.wait()

    far = []
    far_mine = jnp.concatenate([mixed[0, ours, :], mixed[3, ours, :]], axis=0)
    for n in range(chunks):
        cols = pl.ds(n * span, span)
        y = jnp.dot(far_mine, w_out[0, :, cols], preferred_element_type=F32)
        y += jnp.dot(mixed_sib[0:ROWS], w_out[1, :, cols], preferred_element_type=F32)
        far_sum[n] = y.astype(BF16)
        for k, device in enumerate((at(-1, 1), at(1, 0))):
            copy = pltpu.make_async_remote_copy(
                src_ref=far_sum.at[n, pl.ds(k * HALF, HALF)],
                dst_ref=far_in.at[n, ours],
                send_sem=far_send.at[n, k], recv_sem=far_recv.at[n, core],
                device_id=device, device_id_type=MESH,
            )
            copy.start()
            far.append(copy)
    for n in range(chunks):
        cols = pl.ds(n * span, span)
        y = jnp.dot(mixed[1 + core], w_out[0, :, cols], preferred_element_type=F32)
        y += jnp.dot(mixed_sib[ROWS:2 * ROWS], w_out[1, :, cols], preferred_element_type=F32)
        own_sum[n] = y
    moves = []
    for n in range(chunks):
        for k in range(2):
            here = far_in.at[n, pl.ds(k * HALF, HALF)]
            pltpu.make_async_copy(here, here, far_recv.at[n, k]).wait()
        cols = slice(n * span, (n + 1) * span)
        velocity = gate[:, cols] * (own_sum[n] + far_in[n].astype(F32))
        x = state[:, cols]
        moved[n] = (x + sigma_step * velocity).astype(BF16)
        copy = pltpu.make_async_remote_copy(
            src_ref=moved.at[n], dst_ref=moved_in.at[n],
            send_sem=move_send.at[n], recv_sem=move_recv.at[n],
            device_id=at(2, core), device_id_type=MESH,
        )
        copy.start()
        moves.append(copy)
        est[:, cols] = (x - sigma_now * velocity).astype(BF16)
    store_est = pltpu.make_async_copy(est, est_h, store_sem.at[0])
    store_est.start()
    load_noise.wait()
    stores = []
    for n in range(chunks):
        moves[n].wait()
        cols = slice(n * span, (n + 1) * span)
        adv[:, cols] = jnp.where(slot == 0, noise[:, cols].astype(F32), moved_in[n].astype(F32))
        copy = pltpu.make_async_copy(
            adv.at[:, pl.ds(n * span, span)], adv_h.at[:, pl.ds(n * span, span)], store_sem.at[1 + n]
        )
        copy.start()
        stores.append(copy)

    for copy in sends:
        copy.wait_send()
    for n in range(6, 14):
        here = blocks.at[0, pl.ds(0, HALF)]
        pltpu.make_async_copy(here, here, send_sem.at[n]).wait()
    for copy in far:
        copy.wait_send()
    store_est.wait()
    for copy in stores:
        copy.wait()


def on_device(state, noise, modulation, timesteps, plan, frame_ids, w_query, w_key, w_value, w_out):
    rows, width = state.shape
    inner = w_query.shape[1]
    span = 512
    chunks = width // span
    hbm = pl.BlockSpec(memory_space=pl.ANY)
    vmem = pl.BlockSpec(memory_space=pltpu.VMEM)
    smem = pl.BlockSpec(memory_space=pltpu.SMEM)
    dma = pltpu.SemaphoreType.DMA
    advanced, estimate = pl.pallas_call(
        kernel,
        out_shape=(
            jax.ShapeDtypeStruct((rows, width), F32),
            jax.ShapeDtypeStruct((rows, width), BF16),
        ),
        in_specs=[hbm, hbm, vmem, smem, smem, vmem, hbm, hbm, hbm, hbm],
        out_specs=(hbm, hbm),
        scratch_shapes=[
            pltpu.VMEM((rows, width), F32),
            pltpu.VMEM((rows, width), BF16),
            pltpu.VMEM((8, rows, width), BF16),
            pltpu.VMEM((width, 3 * inner), BF16),
            pltpu.VMEM((2, inner, width), BF16),
            pltpu.VMEM((4 * rows, inner), BF16),
            pltpu.VMEM((8 * rows + 32, 2 * inner), BF16),
            pltpu.VMEM((4, rows, 512), F32),
            pltpu.VMEM((4, rows, inner), BF16),
            pltpu.VMEM((2 * rows, inner), BF16),
            pltpu.VMEM((chunks, rows, span), F32),
            pltpu.VMEM((chunks, rows, span), BF16),
            pltpu.VMEM((chunks, rows, span), BF16),
            pltpu.VMEM((chunks, rows, span), BF16),
            pltpu.VMEM((chunks, rows, span), BF16),
            pltpu.VMEM((rows, width), F32),
            pltpu.VMEM((rows, width), BF16),
            dma((6,)),
            dma((1 + chunks,)),
            dma((14,)),
            dma((8, 2)),
            dma((4,)),
            dma((4,)),
            dma((chunks, 2)),
            dma((chunks, 2)),
            dma((chunks,)),
            dma((chunks,)),
        ],
        compiler_params=pltpu.CompilerParams(
            collective_id=0, has_side_effects=True, vmem_limit_bytes=48 << 20
        ),
        name="step",
    )(
        state, noise, modulation, timesteps, plan, frame_ids.reshape(-1, 128),
        w_query, w_key, w_value, w_out,
    )
    return advanced, estimate


def solution(mesh):
    return jax.shard_map(
        on_device,
        mesh=mesh,
        in_specs=(
            P(("queue", "shard"), None),
            P("shard", None),
            P(),
            P("queue"),
            P(),
            P(),
            P(None, "shard"),
            P(None, "shard"),
            P(None, "shard"),
            P("shard", None),
        ),
        out_specs=(P(("queue", "shard"), None), P(("queue", "shard"), None)),
        check_vma=False,
    )
```

```python
import functools

import jax
import jax.numpy as jnp
from jax import lax
from jax.experimental import pallas as pl
from jax.experimental.pallas import tpu as pltpu
from jax.sharding import PartitionSpec as P

MESH = pl.DeviceIdType.MESH
ROWS = 96
HALF = 48
BF16 = jnp.bfloat16
F32 = jnp.float32


def kernel(
    state_h, noise_h, mod_h, step_ref, plan_ref, frame_h, wq_h, wk_h, wv_h, wo_h,
    adv_ref, est_ref,
    state, noise, modulation, frames, blocks, w_in, w_out, queries, kv, bias, mixed, mixed_sib,
    own_sum, far_sum, far_in, next_in, moved, moved_in, pace, pace_in,
    load_sem, send_sem, recv_sem, pair_send, pair_recv,
    far_send, far_recv, next_send, next_recv, extra_send, move_send, move_recv,
):
    width = state.shape[1]
    inner = w_out.shape[1]
    chunks, _, span = own_sum.shape
    slot = lax.axis_index("queue")
    shard = lax.axis_index("shard")
    side = lax.div(shard, 2)
    core = lax.rem(shard, 2)
    other = 1 - core
    last = 2 * lax.axis_size("queue") - 1
    chip = 2 * slot + side

    def at(step, which):
        there = chip + step
        return (lax.div(there, 2), 2 * lax.rem(there, 2) + which)

    sibling = (slot, 2 * side + other)
    has_behind = chip > 0
    has_ahead = chip < last
    low_extra = chip == 1
    high_extra = chip == last - 1

    barrier = pltpu.get_barrier_semaphore()

    def greet(condition, device):
        @pl.when(condition)
        def _():
            pl.semaphore_signal(barrier, inc=1, device_id=device, device_id_type=MESH)

    pl.semaphore_signal(barrier, inc=1, device_id=sibling, device_id_type=MESH)
    greet(has_behind, at(-1, core))
    greet(has_ahead, at(1, core))
    greet(chip >= 2, at(-2, core))
    greet((core == 0) & has_behind, at(-1, 1))
    greet((core == 0) & (chip == 0), at(1, 1))
    greet((core == 0) & (chip >= 3), at(-3, 0))
    greet((core == 0) & (chip >= 3), at(-3, 1))
    greet((core == 1) & has_ahead, at(1, 0))
    greet((core == 1) & (chip >= 2), at(-1, 0))

    def count(condition):
        return jnp.where(condition, 1, 0)

    greeted = (
        1 + count(has_ahead) + count(has_behind)
        + count((core == 0) & has_behind) + count((core == 0) & has_behind & has_ahead)
        + count((core == 1) & has_ahead) + count((core == 1) & low_extra)
        + count(chip <= last - 2) + count(chip <= last - 3)
    )

    def load(source, target, n):
        copy = pltpu.make_async_copy(source, target, load_sem.at[n])
        copy.start()
        return copy

    load_state = [
        load(state_h.at[pl.ds(k * HALF, HALF)], state.at[pl.ds(k * HALF, HALF)], k) for k in range(2)
    ]
    load_mod = load(mod_h, modulation, 2)
    load_frames = load(frame_h, frames, 3)

    level = step_ref[0]
    sigma_now = plan_ref[level]
    sigma_step = plan_ref[level + 1] - sigma_now
    load_mod.wait()
    modulate = modulation[level].astype(F32)
    shift, gain, gate = modulate[0:1], 1.0 + modulate[1:2], modulate[2:3]
    for n in range(ROWS // 16):
        if n % 3 == 0:
            load_state[n // 3].wait()
        rows = pl.ds(n * 16, 16)
        x = state[rows, :]
        x = x - jnp.mean(x, axis=-1, keepdims=True)
        spread = jnp.mean(jnp.square(x), axis=-1, keepdims=True)
        blocks[4 + core, rows, :] = (x * lax.rsqrt(spread + 1e-06) * gain + shift).astype(BF16)
    pl.semaphore_wait(barrier, greeted)

    def send(place, half, to_place, device, n):
        rows = pl.ds(half * HALF, HALF)
        return pltpu.make_async_remote_copy(
            src_ref=blocks.at[place, rows],
            dst_ref=blocks.at[to_place, rows],
            send_sem=send_sem.at[n],
            recv_sem=recv_sem.at[to_place, half],
            device_id=device,
            device_id_type=MESH,
        )

    def wait_block(place, half):
        here = blocks.at[place, pl.ds(half * HALF, HALF)]
        pltpu.make_async_copy(here, here, recv_sem.at[place, half]).wait()

    to_ahead = [send(4 + core, half, 2 + core, at(1, core), half) for half in range(2)]
    to_behind = [send(4 + core, half, 6 + core, at(-1, core), 2 + half) for half in range(2)]
    to_sibling = [send(4 + core, half, 4 + core, sibling, 4 + half) for half in range(2)]
    for half in range(2):
        pl.when(has_ahead)(to_ahead[half].start)
        pl.when(has_behind)(to_behind[half].start)
        to_sibling[half].start()
    load_w = [
        load(w, w_in.at[:, pl.ds(n * inner, inner)], 4 + n)
        for n, w in enumerate((wq_h, wk_h, wv_h))
    ]

    pace[...] = sigma_step * gate
    send_pace = pltpu.make_async_remote_copy(
        src_ref=pace, dst_ref=pace_in, send_sem=pair_send.at[4], recv_sem=pair_recv.at[4],
        device_id=at(2, core), device_id_type=MESH,
    )
    pl.when(chip <= last - 2)(send_pace.start)

    load_frames.wait()
    lines_all = (last + 1) * 192 // 128
    first = 192 * chip - 288 + (last + 1) * 192
    row = lax.div(first, 128)
    line = jnp.concatenate(
        [frames[pl.ds(lax.rem(row + n, lines_all), 1), :] for n in range(7)], axis=1
    ).astype(F32)
    line = jnp.broadcast_to(line, (8, 896))
    line = jnp.where(side == 0, pltpu.roll(line, 896 - 96, 1), pltpu.roll(line, 896 - 32, 1))
    column = jnp.broadcast_to(pltpu.roll(line, 896 - 96, 1)[0:1, :640], (128, 640)).T
    for n in range(4):
        keys = line if n == 0 else pltpu.roll(line, 896 - 96 * n, 1)
        gap = jnp.abs(column[(n + 1) * ROWS:(n + 2) * ROWS, 0:1] - keys[0:1, :512])
        bias[n] = jnp.where(gap <= 1.0, 0.0, -1e30)
    for condition, n, start in ((low_extra, 0, 0), (high_extra, 5, 3)):
        @pl.when(condition)
        def _():
            keys = line if start == 0 else pltpu.roll(line, 896 - 96 * start, 1)
            gap = jnp.abs(column[n * ROWS:(n + 1) * ROWS, 0:1] - keys[0:1, :512])
            bias[4] = jnp.where(gap <= 1.0, 0.0, -1e30)
    kv[pl.ds(8 * ROWS, 32), :] = jnp.zeros((32, 2 * inner), BF16)
    for condition, place in (
        (chip < 2, 1), (chip == 0, 2), (chip == 0, 3),
        (chip == last, 6), (chip == last, 7), (chip > last - 2, 0),
    ):
        @pl.when(condition)
        def _():
            blocks[place] = jnp.zeros((ROWS, width), BF16)

    def gather(parts):
        return jnp.concatenate([blocks[p, r:r + k] for p, r, k in parts], axis=0)

    def project_q(parts, into):
        for n in range(inner // 256):
            y = jnp.dot(gather(parts), w_in[:, n * 256:(n + 1) * 256], preferred_element_type=F32)
            y = y.astype(BF16) * 0.125
            done = 0
            for (_, _, k), r in zip(parts, into):
                queries[r:r + k, n * 256:(n + 1) * 256] = y[done:done + k]
                done += k

    def project_kv(parts, into):
        def part(n, _):
            cols = pl.ds(pl.multiple_of(n * 256, 256), 256)
            w = w_in[:, pl.ds(pl.multiple_of(inner + n * 256, 256), 256)]
            y = jnp.dot(gather(parts), w, preferred_element_type=F32).astype(BF16)
            done = 0
            for (_, _, k), r in zip(parts, into):
                kv[r:r + k, cols] = y[done:done + k]
                done += k
            return 0
        lax.fori_loop(0, 2 * inner // 256, part, 0)

    low = lax.broadcasted_iota(jnp.int32, (ROWS, 128), 1) < 64

    def attend(n, start):
        for g in range(inner // 128):
            q = queries[n * ROWS:(n + 1) * ROWS, g * 128:(g + 1) * 128]
            zero = jnp.zeros_like(q)
            q = jnp.concatenate([jnp.where(low, q, zero), jnp.where(low, zero, q)], axis=0)
            k = kv[start * ROWS:start * ROWS + 512, g * 128:(g + 1) * 128]
            v = kv[start * ROWS:start * ROWS + 512, inner + g * 128:inner + (g + 1) * 128]
            s = lax.dot_general(q, k, (((1,), (1,)), ((), ())), preferred_element_type=F32)
            s = s + jnp.concatenate([bias[n], bias[n]], axis=0)
            w = jnp.exp(s - jnp.max(s, axis=-1, keepdims=True))
            total = jnp.sum(w, axis=-1, keepdims=True)
            o = jnp.dot(w.astype(BF16), v, preferred_element_type=F32) / total
            mixed[n, :, g * 128:(g + 1) * 128] = jnp.where(low, o[:ROWS], o[ROWS:]).astype(BF16)

    for half in range(2):
        wait_block(4 + other, half)
    for copy in load_w:
        copy.wait()
    load_wo = load(wo_h, w_out.at[0], 7)
    load_noise = load(noise_h, noise, 8)
    share_w = pltpu.make_async_remote_copy(
        src_ref=wo_h, dst_ref=w_out.at[1], send_sem=pair_send.at[0], recv_sem=pair_recv.at[0],
        device_id=sibling, device_id_type=MESH,
    )
    share_w.start()
    project_q([(4, 0, 96), (5, 0, 96)], (ROWS, 2 * ROWS))
    project_kv([(4, 0, 96), (5, 0, 96)], (3 * ROWS, 4 * ROWS))

    core_rows = pl.ds(pl.multiple_of(core * HALF, 16), HALF)
    other_rows = pl.ds(pl.multiple_of(other * HALF, 16), HALF)
    both = has_behind & has_ahead

    def forward(place, half, n):
        wait_block(place, half)
        send(place, half, place, sibling, n).start()

    def relay(place, to_place, device, n):
        return pltpu.make_async_remote_copy(
            src_ref=blocks.at[place, core_rows], dst_ref=blocks.at[to_place, core_rows],
            send_sem=send_sem.at[n], recv_sem=recv_sem.at[to_place, core],
            device_id=device, device_id_type=MESH,
        )

    relay_ahead = relay(3, 1, at(1, core), 10)
    relay_behind = relay(6, 0, at(-1, core), 11)

    def when(condition, *steps):
        @pl.when(condition)
        def _():
            for step in steps:
                step()

    def neighbours(half):
        first_core, second_core = core == 0, core == 1
        when(first_core & has_behind, lambda: forward(2, half, 6 + half))
        when(first_core & has_ahead, lambda: forward(6, half, 8 + half))
        when(second_core & has_behind, lambda: forward(3, half, 6 + half))
        if half == 1:
            when(second_core & both, relay_ahead.start)
        else:
            when(first_core & both, relay_behind.start)
        when(second_core & has_ahead, lambda: forward(7, half, 8 + half))
        when(first_core & has_behind, lambda: wait_block(3, half))
        if half == 0:
            when(first_core & both, relay_ahead.start)
        when(first_core & has_ahead, lambda: wait_block(7, half))
        when(second_core & has_ahead, lambda: wait_block(6, half))
        if half == 1:
            when(second_core & both, relay_behind.start)
        when(second_core & has_behind, lambda: wait_block(2, half))
        r = half * HALF
        project_q([(3, r, HALF), (6, r, HALF)], (r, 3 * ROWS + r))
        project_kv(
            [(2, r, HALF), (3, r, HALF), (6, r, HALF), (7, r, HALF)],
            (ROWS + r, 2 * ROWS + r, 5 * ROWS + r, 6 * ROWS + r),
        )

    neighbours(0)
    neighbours(1)
    attend(1, 1)
    attend(2, 2)

    def swap(source, start, rows, n):
        return pltpu.make_async_remote_copy(
            src_ref=source, dst_ref=mixed_sib.at[pl.ds(start, rows)],
            send_sem=pair_send.at[n], recv_sem=pair_recv.at[n],
            device_id=sibling, device_id_type=MESH,
        )

    swap_own = swap(mixed.at[1 + other], ROWS, ROWS, 1)
    swap_own.start()

    def forward_far(k):
        here = blocks.at[k, core_rows]
        pltpu.make_async_copy(here, here, recv_sem.at[k, core]).wait()
        pltpu.make_async_remote_copy(
            src_ref=here, dst_ref=here, send_sem=send_sem.at[12 + k],
            recv_sem=recv_sem.at[k, core], device_id=sibling, device_id_type=MESH,
        ).start()

    def wait_far(k):
        here = blocks.at[k, other_rows]
        pltpu.make_async_copy(here, here, recv_sem.at[k, other]).wait()

    when(chip >= 2, lambda: forward_far(1))
    when(chip <= last - 2, lambda: forward_far(0))

    load_wo.wait()
    share_w.wait()
    swap_own.wait()
    moves = []
    for n in range(chunks):
        cols = slice(n * span, (n + 1) * span)
        y = jnp.dot(mixed[1 + core], w_out[0, :, cols], preferred_element_type=F32)
        y += jnp.dot(mixed_sib[ROWS:2 * ROWS], w_out[1, :, cols], preferred_element_type=F32)
        own_sum[n] = y
        moved[n] = (state[:, cols] + sigma_step * gate[:, cols] * y).astype(BF16)
        moves.append(pltpu.make_async_remote_copy(
            src_ref=moved.at[n], dst_ref=moved_in.at[n],
            send_sem=move_send.at[n], recv_sem=move_recv.at[n],
            device_id=at(2, core), device_id_type=MESH,
        ))
        pl.when(chip <= last - 2)(moves[n].start)

    def project_out(mine, theirs, n):
        cols = slice(n * span, (n + 1) * span)
        y = jnp.dot(mine, w_out[0, :, cols], preferred_element_type=F32)
        y += jnp.dot(theirs, w_out[1, :, cols], preferred_element_type=F32)
        return y.astype(BF16)

    def give(source, target, n, half, device, send, recv):
        return pltpu.make_async_remote_copy(
            src_ref=source, dst_ref=target.at[n, core_rows],
            send_sem=send, recv_sem=recv.at[n, core],
            device_id=device, device_id_type=MESH,
        )

    swap_extra = swap(mixed.at[4, other_rows], 2 * ROWS, HALF, 5)
    third = pl.ds(ROWS, HALF)

    def extra(n, device):
        return give(far_sum.at[n, third], far_in, n, 2, device, extra_send.at[n, 0], far_recv)

    def extra_next(n):
        return give(far_sum.at[n, third], next_in, n, 2, at(1, 0), extra_send.at[n, 1], next_recv)

    when(low_extra, lambda: project_q([(2, 0, ROWS)], (4 * ROWS,)), lambda: attend(4, 0))
    when(high_extra, lambda: project_q([(7, 0, ROWS)], (4 * ROWS,)), lambda: attend(4, 3))

    @pl.when(low_extra | high_extra)
    def _():
        swap_extra.start()
        swap_extra.wait()
        for n in range(chunks):
            far_sum[n, third] = project_out(mixed[4, core_rows], mixed_sib[2 * ROWS:2 * ROWS + HALF], n)
            when(low_extra, extra(n, at(-1, 0)).start, extra_next(n).start)
            when(high_extra, extra(n, at(1, 1)).start)

    when(chip >= 2, lambda: wait_far(1))
    when(chip <= last - 2, lambda: wait_far(0))
    project_kv([(0, 0, ROWS), (1, 0, ROWS)], (7 * ROWS, 0))
    attend(0, 0)
    swap_low = swap(mixed.at[0, other_rows], 0, HALF, 2)
    swap_low.start()
    attend(3, 3)
    swap_high = swap(mixed.at[3, other_rows], HALF, HALF, 3)
    swap_high.start()
    swap_low.wait()
    swap_high.wait()

    far = []
    far_mine = jnp.concatenate([mixed[0, core_rows, :], mixed[3, core_rows, :]], axis=0)
    for n in range(chunks):
        far_sum[n, 0:ROWS] = project_out(far_mine, mixed_sib[0:ROWS], n)
        below, above = far_sum.at[n, pl.ds(0, HALF)], far_sum.at[n, pl.ds(HALF, HALF)]
        group = (
            (has_behind, give(below, far_in, n, 0, at(-1, 1), far_send.at[n, 0], far_recv)),
            (has_ahead, give(above, far_in, n, 1, at(1, 0), far_send.at[n, 1], far_recv)),
            (both, give(below, next_in, n, 0, at(1, 1), next_send.at[n, 0], next_recv)),
            (chip <= last - 3, give(above, next_in, n, 1, at(3, 0), next_send.at[n, 1], next_recv)),
        )
        for condition, copy in group:
            pl.when(condition)(copy.start)
        far.extend(group)

    def wait_halves(target, n, sem):
        for k in range(2):
            here = target.at[n, pl.ds(k * HALF, HALF)]
            pltpu.make_async_copy(here, here, sem.at[n, k]).wait()

    load_noise.wait()

    @pl.when(slot == 0)
    def _():
        adv_ref[...] = noise[...].astype(F32)

    when(slot > 0, send_pace.wait_recv)
    for n in range(chunks):
        cols = slice(n * span, (n + 1) * span)
        wait_halves(far_in, n, far_recv)
        velocity = gate[:, cols] * (own_sum[n] + far_in[n].astype(F32))
        est_ref[:, cols] = (state[:, cols] - sigma_now * velocity).astype(BF16)

        @pl.when(slot > 0)
        def _():
            moves[n].wait_recv()
            wait_halves(next_in, n, next_recv)
            adv_ref[:, cols] = moved_in[n].astype(F32) + pace_in[:, cols] * next_in[n].astype(F32)

    def left(condition, n):
        here = blocks.at[0, pl.ds(0, HALF)]
        when(condition, lambda: pltpu.make_async_copy(here, here, send_sem.at[n]).wait())

    for half in range(2):
        left(has_ahead, half)
        left(has_behind, 2 + half)
        left(chip >= 0, 4 + half)
        left(has_behind, 6 + half)
        left(has_ahead, 8 + half)
    left(both, 10)
    left(both, 11)
    left(chip <= last - 2, 12)
    left(chip >= 2, 13)
    for condition, copy in far:
        when(condition, copy.wait_send)
    when(chip <= last - 2, send_pace.wait_send, *[copy.wait_send for copy in moves])
    for n in range(chunks):
        when(low_extra, extra(n, at(-1, 0)).wait_send, extra_next(n).wait_send)
        when(high_extra, extra(n, at(1, 1)).wait_send)


def on_device(state, noise, modulation, timesteps, plan, frame_ids, w_query, w_key, w_value, w_out):
    rows, width = state.shape
    inner = w_query.shape[1]
    span = 512
    chunks = width // span
    hbm = pl.BlockSpec(memory_space=pltpu.HBM)
    vmem = pl.BlockSpec(memory_space=pltpu.VMEM)
    smem = pl.BlockSpec(memory_space=pltpu.SMEM)
    dma = pltpu.SemaphoreType.DMA
    advanced, estimate = pl.pallas_call(
        kernel,
        out_shape=(
            jax.ShapeDtypeStruct((rows, width), F32),
            jax.ShapeDtypeStruct((rows, width), BF16),
        ),
        in_specs=[hbm, hbm, hbm, smem, smem, hbm, hbm, hbm, hbm, hbm],
        out_specs=(vmem, vmem),
        scratch_shapes=[
            pltpu.VMEM((rows, width), F32),
            pltpu.VMEM((rows, width), BF16),
            pltpu.VMEM(modulation.shape, BF16),
            pltpu.VMEM((frame_ids.size // 128, 128), jnp.int32),
            pltpu.VMEM((8, rows, width), BF16),
            pltpu.VMEM((width, 3 * inner), BF16),
            pltpu.VMEM((2, inner, width), BF16),
            pltpu.VMEM((5 * rows, inner), BF16),
            pltpu.VMEM((8 * rows + 32, 2 * inner), BF16),
            pltpu.VMEM((5, rows, 512), F32),
            pltpu.VMEM((5, rows, inner), BF16),
            pltpu.VMEM((3 * rows, inner), BF16),
            pltpu.VMEM((chunks, rows, span), F32),
            pltpu.VMEM((chunks, rows + HALF, span), BF16),
            pltpu.VMEM((chunks, rows, span), BF16),
            pltpu.VMEM((chunks, rows, span), BF16),
            pltpu.VMEM((chunks, rows, span), BF16),
            pltpu.VMEM((chunks, rows, span), BF16),
            pltpu.VMEM((1, width), F32),
            pltpu.VMEM((1, width), F32),
            dma((9,)),
            dma((14,)),
            dma((8, 2)),
            dma((6,)),
            dma((6,)),
            dma((chunks, 2)),
            dma((chunks, 2)),
            dma((chunks, 2)),
            dma((chunks, 2)),
            dma((chunks, 2)),
            dma((chunks,)),
            dma((chunks,)),
        ],
        compiler_params=pltpu.CompilerParams(
            collective_id=0, has_side_effects=True, vmem_limit_bytes=62914560
        ),
        name="step",
    )(
        state, noise, modulation, timesteps, plan, frame_ids.reshape(-1, 128),
        w_query, w_key, w_value, w_out,
    )
    return advanced, estimate


def solution(mesh):
    return jax.shard_map(
        on_device,
        mesh=mesh,
        in_specs=(
            P(("queue", "shard"), None),
            P("shard", None),
            P(),
            P("queue"),
            P(),
            P(),
            P(None, "shard"),
            P(None, "shard"),
            P(None, "shard"),
            P("shard", None),
        ),
        out_specs=(P(("queue", "shard"), None), P(("queue", "shard"), None)),
        check_vma=False,
    )
```

```python
import functools

import jax
import jax.numpy as jnp
from jax import lax
from jax.experimental import pallas as pl
from jax.experimental.pallas import tpu as pltpu
from jax.sharding import PartitionSpec as P

MESH = pl.DeviceIdType.MESH
ROWS = 96
HALF = 48
BF16 = jnp.bfloat16
F32 = jnp.float32


def kernel(
    state_h, noise_h, mod_h, step_ref, plan_ref, frame_h, wq_h, wk_h, wv_h, wo_h,
    adv_ref, est_ref,
    state, noise, modulation, frames, blocks, w_in, w_out, queries, kv, bias, mixed, mixed_sib,
    own_sum, far_sum, far_in, next_out, next_in, passing, moved, moved_in, pace,
    load_sem, send_sem, recv_sem, pair_send, pair_recv,
    far_send, far_recv, next_send, next_recv, extra_send, move_send, move_recv, pace_send, pace_recv, pass_send, pass_recv,
):
    width = state.shape[1]
    inner = w_out.shape[1]
    chunks, _, span = own_sum.shape
    slot = lax.axis_index("queue")
    shard = lax.axis_index("shard")
    side = lax.div(shard, 2)
    core = lax.rem(shard, 2)
    other = 1 - core
    last = 2 * lax.axis_size("queue") - 1
    chip = 2 * slot + side

    def at(step, which):
        there = chip + step
        return (lax.div(there, 2), 2 * lax.rem(there, 2) + which)

    sibling = (slot, 2 * side + other)
    turn = lax.rem(chip, 4)
    detour = (turn == 3) & (chip <= last - 3)
    relays = (turn == 2) & (chip <= last - 4)
    has_behind = chip > 0
    has_ahead = chip < last
    low_extra = chip == 1
    high_extra = chip == last - 1

    barrier = pltpu.get_barrier_semaphore()

    def greet(condition, device):
        @pl.when(condition)
        def _():
            pl.semaphore_signal(barrier, inc=1, device_id=device, device_id_type=MESH)

    pl.semaphore_signal(barrier, inc=1, device_id=sibling, device_id_type=MESH)
    greet(has_behind, at(-1, core))
    greet(has_ahead, at(1, core))
    greet((core == 0) & has_behind, at(-1, 1))
    greet((core == 0) & (chip == 0), at(1, 1))
    for k in range(2):
        greet((core == 0) & (chip >= 3), at(jnp.where(turn == 2, -4, -3), k))
    greet((core == 1) & has_ahead, at(1, 0))
    greet((core == 1) & has_behind, at(-1, 0))

    def count(condition):
        return jnp.where(condition, 1, 0)

    greeted = (
        1 + count(has_ahead) + count(has_behind)
        + count((core == 0) & has_behind) + count((core == 0) & has_ahead)
        + count((core == 1) & has_ahead) + count((core == 1) & low_extra)
        + count((chip <= last - 3) & (turn != 3)) + count(relays)
    )

    def load(source, target, n):
        copy = pltpu.make_async_copy(source, target, load_sem.at[n])
        copy.start()
        return copy

    load_state = [
        load(state_h.at[pl.ds(k * HALF, HALF)], state.at[pl.ds(k * HALF, HALF)], k) for k in range(2)
    ]
    load_mod = load(mod_h, modulation, 2)
    load_frames = load(frame_h, frames, 3)

    level = step_ref[0]
    sigma_now = plan_ref[level]
    sigma_step = plan_ref[level + 1] - sigma_now
    load_mod.wait()
    modulate = modulation[level].astype(F32)
    shift, gain, gate = modulate[0:1], 1.0 + modulate[1:2], modulate[2:3]
    for n in range(ROWS // 16):
        if n % 3 == 0:
            load_state[n // 3].wait()
        rows = pl.ds(n * 16, 16)
        x = state[rows, :]
        x = x - jnp.mean(x, axis=-1, keepdims=True)
        spread = jnp.mean(jnp.square(x), axis=-1, keepdims=True)
        blocks[4 + core, rows, :] = (x * lax.rsqrt(spread + 1e-06) * gain + shift).astype(BF16)
    pl.semaphore_wait(barrier, greeted)

    def send(place, half, to_place, device, n):
        rows = pl.ds(half * HALF, HALF)
        return pltpu.make_async_remote_copy(
            src_ref=blocks.at[place, rows],
            dst_ref=blocks.at[to_place, rows],
            send_sem=send_sem.at[n],
            recv_sem=recv_sem.at[to_place, half],
            device_id=device,
            device_id_type=MESH,
        )

    def wait_block(place, half):
        here = blocks.at[place, pl.ds(half * HALF, HALF)]
        pltpu.make_async_copy(here, here, recv_sem.at[place, half]).wait()

    to_ahead = [send(4 + core, half, 2 + core, at(1, core), half) for half in range(2)]
    to_behind = [send(4 + core, half, 6 + core, at(-1, core), 2 + half) for half in range(2)]
    to_sibling = [send(4 + core, half, 4 + core, sibling, 4 + half) for half in range(2)]
    for half in range(2):
        pl.when(has_ahead)(to_ahead[half].start)
        pl.when(has_behind)(to_behind[half].start)
        to_sibling[half].start()
    load_w = [
        load(w, w_in.at[:, pl.ds(n * inner, inner)], 4 + n)
        for n, w in enumerate((wq_h, wk_h, wv_h))
    ]

    pace[0] = sigma_step * gate
    step = 2 * core - 1
    paces = [
        pltpu.make_async_remote_copy(
            src_ref=pace.at[0], dst_ref=pace.at[2 - core],
            send_sem=pace_send.at[k], recv_sem=pace_recv.at[1 - core],
            device_id=at(step, k), device_id_type=MESH,
        )
        for k in range(2)
    ]
    gives = chip <= last - 2
    gives_pace = gives & ((core == 1) | has_behind)
    for copy in paces:
        pl.when(gives_pace)(copy.start)

    load_frames.wait()
    lines_all = (last + 1) * 192 // 128
    first = 192 * chip - 288 + (last + 1) * 192
    row = lax.div(first, 128)
    line = jnp.concatenate(
        [frames[pl.ds(lax.rem(row + n, lines_all), 1), :] for n in range(7)], axis=1
    ).astype(F32)
    line = jnp.broadcast_to(line, (8, 896))
    line = jnp.where(side == 0, pltpu.roll(line, 896 - 96, 1), pltpu.roll(line, 896 - 32, 1))
    column = jnp.broadcast_to(pltpu.roll(line, 896 - 96, 1)[0:1, :640], (128, 640)).T
    for n in range(4):
        keys = line if n == 0 else pltpu.roll(line, 896 - 96 * n, 1)
        gap = jnp.abs(column[(n + 1) * ROWS:(n + 2) * ROWS, 0:1] - keys[0:1, :512])
        bias[n] = jnp.where(gap <= 1.0, 0.0, -1e30)
    for condition, n, start in ((low_extra, 0, 0), (high_extra, 5, 3)):
        @pl.when(condition)
        def _():
            keys = line if start == 0 else pltpu.roll(line, 896 - 96 * start, 1)
            gap = jnp.abs(column[n * ROWS:(n + 1) * ROWS, 0:1] - keys[0:1, :512])
            bias[4] = jnp.where(gap <= 1.0, 0.0, -1e30)
    kv[pl.ds(8 * ROWS, 32), :] = jnp.zeros((32, 2 * inner), BF16)
    for condition, place in (
        (chip < 2, 1), (chip == 0, 2), (chip == 0, 3),
        (chip == last, 6), (chip == last, 7), (chip > last - 2, 0),
    ):
        @pl.when(condition)
        def _():
            blocks[place] = jnp.zeros((ROWS, width), BF16)

    def gather(parts):
        return jnp.concatenate([blocks[p, r:r + k] for p, r, k in parts], axis=0)

    def project_q(parts, into):
        for n in range(inner // 256):
            y = jnp.dot(gather(parts), w_in[:, n * 256:(n + 1) * 256], preferred_element_type=F32)
            y = y.astype(BF16) * 0.125
            done = 0
            for (_, _, k), r in zip(parts, into):
                queries[r:r + k, n * 256:(n + 1) * 256] = y[done:done + k]
                done += k

    def project_kv(parts, into):
        def part(n, _):
            cols = pl.ds(pl.multiple_of(n * 256, 256), 256)
            w = w_in[:, pl.ds(pl.multiple_of(inner + n * 256, 256), 256)]
            y = jnp.dot(gather(parts), w, preferred_element_type=F32).astype(BF16)
            done = 0
            for (_, _, k), r in zip(parts, into):
                kv[r:r + k, cols] = y[done:done + k]
                done += k
            return 0
        lax.fori_loop(0, 2 * inner // 256, part, 0)

    low = lax.broadcasted_iota(jnp.int32, (ROWS, 128), 1) < 64

    def attend(n, start):
        for g in range(inner // 128):
            q = queries[n * ROWS:(n + 1) * ROWS, g * 128:(g + 1) * 128]
            zero = jnp.zeros_like(q)
            q = jnp.concatenate([jnp.where(low, q, zero), jnp.where(low, zero, q)], axis=0)
            k = kv[start * ROWS:start * ROWS + 512, g * 128:(g + 1) * 128]
            v = kv[start * ROWS:start * ROWS + 512, inner + g * 128:inner + (g + 1) * 128]
            s = lax.dot_general(q, k, (((1,), (1,)), ((), ())), preferred_element_type=F32)
            s = s + jnp.concatenate([bias[n], bias[n]], axis=0)
            w = jnp.exp(s - jnp.max(s, axis=-1, keepdims=True))
            total = jnp.sum(w, axis=-1, keepdims=True)
            o = jnp.dot(w.astype(BF16), v, preferred_element_type=F32) / total
            mixed[n, :, g * 128:(g + 1) * 128] = jnp.where(low, o[:ROWS], o[ROWS:]).astype(BF16)

    for half in range(2):
        wait_block(4 + other, half)
    for copy in load_w:
        copy.wait()
    load_wo = load(wo_h, w_out.at[0], 7)
    load_noise = load(noise_h, noise, 8)
    share_w = pltpu.make_async_remote_copy(
        src_ref=wo_h, dst_ref=w_out.at[1], send_sem=pair_send.at[0], recv_sem=pair_recv.at[0],
        device_id=sibling, device_id_type=MESH,
    )
    share_w.start()
    project_q([(4, 0, 96), (5, 0, 96)], (ROWS, 2 * ROWS))
    project_kv([(4, 0, 96), (5, 0, 96)], (3 * ROWS, 4 * ROWS))

    core_rows = pl.ds(pl.multiple_of(core * HALF, 16), HALF)
    other_rows = pl.ds(pl.multiple_of(other * HALF, 16), HALF)
    both = has_behind & has_ahead

    def forward(place, half, n):
        wait_block(place, half)
        send(place, half, place, sibling, n).start()

    def relay(place, to_place, device, n):
        return pltpu.make_async_remote_copy(
            src_ref=blocks.at[place, core_rows], dst_ref=blocks.at[to_place, core_rows],
            send_sem=send_sem.at[n], recv_sem=recv_sem.at[to_place, core],
            device_id=device, device_id_type=MESH,
        )

    relay_ahead = relay(3, 1, at(1, core), 10)
    relay_behind = relay(6, 0, at(-1, core), 11)

    def when(condition, *steps):
        @pl.when(condition)
        def _():
            for step in steps:
                step()

    def neighbours(half):
        first_core, second_core = core == 0, core == 1
        when(first_core & has_behind, lambda: forward(2, half, 6 + half))
        when(first_core & has_ahead, lambda: forward(6, half, 8 + half))
        when(second_core & has_behind, lambda: forward(3, half, 6 + half))
        if half == 1:
            when(second_core & both, relay_ahead.start)
        else:
            when(first_core & both, relay_behind.start)
        when(second_core & has_ahead, lambda: forward(7, half, 8 + half))
        when(first_core & has_behind, lambda: wait_block(3, half))
        if half == 0:
            when(first_core & both, relay_ahead.start)
        when(first_core & has_ahead, lambda: wait_block(7, half))
        when(second_core & has_ahead, lambda: wait_block(6, half))
        if half == 1:
            when(second_core & both, relay_behind.start)
        when(second_core & has_behind, lambda: wait_block(2, half))
        r = half * HALF
        project_q([(3, r, HALF), (6, r, HALF)], (r, 3 * ROWS + r))
        project_kv(
            [(2, r, HALF), (3, r, HALF), (6, r, HALF), (7, r, HALF)],
            (ROWS + r, 2 * ROWS + r, 5 * ROWS + r, 6 * ROWS + r),
        )

    neighbours(0)
    neighbours(1)
    attend(1, 1)
    attend(2, 2)

    def swap(source, start, rows, n):
        return pltpu.make_async_remote_copy(
            src_ref=source, dst_ref=mixed_sib.at[pl.ds(start, rows)],
            send_sem=pair_send.at[n], recv_sem=pair_recv.at[n],
            device_id=sibling, device_id_type=MESH,
        )

    swap_own = swap(mixed.at[1 + other], ROWS, ROWS, 1)
    swap_own.start()

    def forward_far(k):
        here = blocks.at[k, core_rows]
        pltpu.make_async_copy(here, here, recv_sem.at[k, core]).wait()
        pltpu.make_async_remote_copy(
            src_ref=here, dst_ref=here, send_sem=send_sem.at[12 + k],
            recv_sem=recv_sem.at[k, core], device_id=sibling, device_id_type=MESH,
        ).start()

    def wait_far(k):
        here = blocks.at[k, other_rows]
        pltpu.make_async_copy(here, here, recv_sem.at[k, other]).wait()

    when(chip >= 2, lambda: forward_far(1))
    when(chip <= last - 2, lambda: forward_far(0))

    load_wo.wait()
    share_w.wait()
    swap_own.wait()
    moves = []
    low_end = (chip == 0) & (core == 0)
    which = jnp.where(low_end, 2, 1 - core)
    place = pl.multiple_of(which * HALF, 16)
    for n in range(chunks):
        cols = slice(n * span, (n + 1) * span)
        y = jnp.dot(mixed[1 + core], w_out[0, :, cols], preferred_element_type=F32)
        y += jnp.dot(mixed_sib[ROWS:2 * ROWS], w_out[1, :, cols], preferred_element_type=F32)
        own_sum[n] = y
        moved[n] = (state[:, cols] + pace[0, :, cols] * y).astype(BF16)
        for k in range(2):
            copy = pltpu.make_async_remote_copy(
                src_ref=moved.at[n, pl.ds(k * HALF, HALF)], dst_ref=moved_in.at[n, pl.ds(place, HALF)],
                send_sem=move_send.at[n, k],
                recv_sem=move_recv.at[n, which],
                device_id=at(jnp.where(low_end, 1, step), k), device_id_type=MESH,
            )
            pl.when(gives)(copy.start)
            moves.append(copy)

    def wait_moved(condition, n, k):
        here = moved_in.at[n, pl.ds(k * HALF, HALF)]
        when(condition, lambda: pltpu.make_async_copy(here, here, move_recv.at[n, k]).wait())

    def project_out(mine, theirs, n):
        cols = slice(n * span, (n + 1) * span)
        y = jnp.dot(mine, w_out[0, :, cols], preferred_element_type=F32)
        y += jnp.dot(theirs, w_out[1, :, cols], preferred_element_type=F32)
        return y

    def give(source, target, n, half, device, send, recv):
        return pltpu.make_async_remote_copy(
            src_ref=source, dst_ref=target.at[n, core_rows],
            send_sem=send, recv_sem=recv.at[n, core],
            device_id=device, device_id_type=MESH,
        )

    swap_extra = swap(mixed.at[4, other_rows], 2 * ROWS, HALF, 5)
    third = pl.ds(ROWS, HALF)

    def extra(n, device):
        return give(far_sum.at[n, third], far_in, n, 2, device, extra_send.at[n, 0], far_recv)

    def extra_next(n):
        return give(next_out.at[n, third], next_in, n, 2, at(1, 0), extra_send.at[n, 1], next_recv)

    when(low_extra, lambda: project_q([(2, 0, ROWS)], (4 * ROWS,)), lambda: attend(4, 0))
    when(high_extra, lambda: project_q([(7, 0, ROWS)], (4 * ROWS,)), lambda: attend(4, 3))

    when(low_extra | high_extra, swap_extra.start)
    when(chip >= 2, lambda: wait_far(1))
    when(chip <= last - 2, lambda: wait_far(0))
    project_kv([(0, 0, ROWS), (1, 0, ROWS)], (7 * ROWS, 0))
    attend(0, 0)
    swap_low = swap(mixed.at[0, other_rows], 0, HALF, 2)
    swap_low.start()
    attend(3, 3)
    swap_high = swap(mixed.at[3, other_rows], HALF, HALF, 3)
    swap_high.start()
    swap_low.wait()
    swap_high.wait()

    for condition, k in ((both, 0), (chip <= last - 3, 1)):
        here = pace.at[1 + k]
        when(condition, pltpu.make_async_copy(here, here, pace_recv.at[k]).wait)
    far = []
    far_mine = jnp.concatenate([mixed[0, core_rows, :], mixed[3, core_rows, :]], axis=0)
    for n in range(chunks):
        cols = slice(n * span, (n + 1) * span)
        y = project_out(far_mine, mixed_sib[0:ROWS], n)
        far_sum[n, 0:ROWS] = y.astype(BF16)
        wait_moved(both, n, 0)
        wait_moved(chip <= last - 3, n, 1)
        for k in range(2):
            rows = pl.ds(k * HALF, HALF)
            base = moved_in[n, rows].astype(F32)
            next_out[n, rows] = (base + pace[1 + k, :, cols] * y[k * HALF:(k + 1) * HALF]).astype(BF16)
        below, above = far_sum.at[n, pl.ds(0, HALF)], far_sum.at[n, pl.ds(HALF, HALF)]
        next_below, next_above = next_out.at[n, pl.ds(0, HALF)], next_out.at[n, pl.ds(HALF, HALF)]
        group = (
            (has_behind, give(below, far_in, n, 0, at(-1, 1), far_send.at[n, 0], far_recv)),
            (has_ahead, give(above, far_in, n, 1, at(1, 0), far_send.at[n, 1], far_recv)),
            (both, give(next_below, next_in, n, 0, at(1, 1), next_send.at[n, 0], next_recv)),
            ((chip <= last - 3) & (turn != 3), give(next_above, next_in, n, 1, at(3, 0), next_send.at[n, 1], next_recv)),
            (detour, pltpu.make_async_remote_copy(
                src_ref=next_above, dst_ref=passing.at[n], send_sem=next_send.at[n, 1],
                recv_sem=pass_recv.at[n], device_id=at(-1, core), device_id_type=MESH,
            )),
        )
        for condition, copy in group:
            pl.when(condition)(copy.start)
        far.extend(group)

    @pl.when(low_extra | high_extra)
    def _():
        swap_extra.wait()
        for n in range(chunks):
            cols = slice(n * span, (n + 1) * span)
            y = project_out(mixed[4, core_rows], mixed_sib[2 * ROWS:2 * ROWS + HALF], n)
            far_sum[n, third] = y.astype(BF16)
            wait_moved(low_extra, n, 2)
            base = moved_in[n, third].astype(F32)
            next_out[n, third] = (base + pace[0, :, cols] * y).astype(BF16)
            when(low_extra, extra(n, at(-1, 0)).start, extra_next(n).start)
            when(high_extra, extra(n, at(1, 1)).start)

    def wait_halves(target, n, sem):
        for k in range(2):
            here = target.at[n, pl.ds(k * HALF, HALF)]
            pltpu.make_async_copy(here, here, sem.at[n, k]).wait()

    def onward(n):
        return give(passing.at[n], next_in, n, 1, at(4, 0), pass_send.at[n], next_recv)

    def pass_on(n):
        pltpu.make_async_copy(passing.at[n], passing.at[n], pass_recv.at[n]).wait()
        onward(n).start()

    when(relays, *[functools.partial(pass_on, n) for n in range(chunks)])
    load_noise.wait()

    @pl.when(slot == 0)
    def _():
        adv_ref[...] = noise[...].astype(F32)

    for n in range(chunks):
        cols = slice(n * span, (n + 1) * span)
        wait_halves(far_in, n, far_recv)
        velocity = gate[:, cols] * (own_sum[n] + far_in[n].astype(F32))
        est_ref[:, cols] = (state[:, cols] - sigma_now * velocity).astype(BF16)

        @pl.when(slot > 0)
        def _():
            wait_halves(next_in, n, next_recv)
            adv_ref[:, cols] = next_in[n].astype(F32)

    def left(condition, n):
        here = blocks.at[0, pl.ds(0, HALF)]
        when(condition, lambda: pltpu.make_async_copy(here, here, send_sem.at[n]).wait())

    for half in range(2):
        left(has_ahead, half)
        left(has_behind, 2 + half)
        left(chip >= 0, 4 + half)
        left(has_behind, 6 + half)
        left(has_ahead, 8 + half)
    left(both, 10)
    left(both, 11)
    left(chip <= last - 2, 12)
    left(chip >= 2, 13)
    for condition, copy in far:
        when(condition, copy.wait_send)
    for n in range(chunks):
        when(relays, onward(n).wait_send)
    when(gives_pace, *[copy.wait_send for copy in paces])
    when(gives, *[copy.wait_send for copy in moves])
    for n in range(chunks):
        when(low_extra, extra(n, at(-1, 0)).wait_send, extra_next(n).wait_send)
        when(high_extra, extra(n, at(1, 1)).wait_send)


def finish(adv_in, est_in, adv_out, est_out, sem):
    copies = [
        pltpu.make_async_copy(adv_in, adv_out, sem.at[0]), pltpu.make_async_copy(est_in, est_out, sem.at[1])
    ]
    for copy in copies:
        copy.start()
    for copy in copies:
        copy.wait()


def on_device(state, noise, modulation, timesteps, plan, frame_ids, w_query, w_key, w_value, w_out):
    rows, width = state.shape
    inner = w_query.shape[1]
    span = 512
    chunks = width // span
    hbm = pl.BlockSpec(memory_space=pltpu.HBM)
    vmem = pl.BlockSpec(memory_space=pltpu.VMEM)
    smem = pl.BlockSpec(memory_space=pltpu.SMEM)
    dma = pltpu.SemaphoreType.DMA
    advanced, estimate = pl.pallas_call(
        kernel,
        out_shape=(
            jax.ShapeDtypeStruct((rows, width), F32),
            jax.ShapeDtypeStruct((rows, width), BF16),
        ),
        in_specs=[hbm, hbm, hbm, smem, smem, hbm, hbm, hbm, hbm, hbm],
        out_specs=(vmem, vmem),
        scratch_shapes=[
            pltpu.VMEM((rows, width), F32),
            pltpu.VMEM((rows, width), BF16),
            pltpu.VMEM(modulation.shape, BF16),
            pltpu.VMEM((frame_ids.size // 128, 128), jnp.int32),
            pltpu.VMEM((8, rows, width), BF16),
            pltpu.VMEM((width, 3 * inner), BF16),
            pltpu.VMEM((2, inner, width), BF16),
            pltpu.VMEM((5 * rows, inner), BF16),
            pltpu.VMEM((8 * rows + 32, 2 * inner), BF16),
            pltpu.VMEM((5, rows, 512), F32),
            pltpu.VMEM((5, rows, inner), BF16),
            pltpu.VMEM((3 * rows, inner), BF16),
            pltpu.VMEM((chunks, rows, span), F32),
            pltpu.VMEM((chunks, rows + HALF, span), BF16),
            pltpu.VMEM((chunks, rows, span), BF16),
            pltpu.VMEM((chunks, rows + HALF, span), BF16),
            pltpu.VMEM((chunks, rows, span), BF16),
            pltpu.VMEM((chunks, HALF, span), BF16),
            pltpu.VMEM((chunks, rows, span), BF16),
            pltpu.VMEM((chunks, rows + HALF, span), BF16),
            pltpu.VMEM((3, 1, width), F32),
            dma((9,)),
            dma((14,)),
            dma((8, 2)),
            dma((6,)),
            dma((6,)),
            dma((chunks, 2)),
            dma((chunks, 2)),
            dma((chunks, 2)),
            dma((chunks, 2)),
            dma((chunks, 2)),
            dma((chunks, 2)),
            dma((chunks, 3)),
            dma((2,)),
            dma((2,)),
            dma((chunks,)),
            dma((chunks,)),
        ],
        compiler_params=pltpu.CompilerParams(
            collective_id=0, has_side_effects=True, vmem_limit_bytes=62914560
        ),
        name="step",
    )(
        state, noise, modulation, timesteps, plan, frame_ids.reshape(-1, 128),
        w_query, w_key, w_value, w_out,
    )
    return pl.pallas_call(
        finish,
        out_shape=(
            jax.ShapeDtypeStruct((rows, width), F32),
            jax.ShapeDtypeStruct((rows, width), BF16),
        ),
        in_specs=[vmem, vmem],
        out_specs=(hbm, hbm),
        scratch_shapes=[dma((2,))],
        name="finish",
    )(advanced, estimate)


def solution(mesh):
    return jax.shard_map(
        on_device,
        mesh=mesh,
        in_specs=(
            P(("queue", "shard"), None),
            P("shard", None),
            P(),
            P("queue"),
            P(),
            P(),
            P(None, "shard"),
            P(None, "shard"),
            P(None, "shard"),
            P("shard", None),
        ),
        out_specs=(P(("queue", "shard"), None), P(("queue", "shard"), None)),
        check_vma=False,
    )
```

```python
import functools

import jax
import jax.numpy as jnp
from jax import lax
from jax.experimental import pallas as pl
from jax.experimental.pallas import tpu as pltpu
from jax.sharding import PartitionSpec as P

MESH = pl.DeviceIdType.MESH
ROWS = 96
HALF = 48
BF16 = jnp.bfloat16
F32 = jnp.float32


def kernel(
    state_h, noise_h, mod_h, step_ref, plan_ref, frame_h, wq_h, wk_h, wv_h, wo_h,
    adv_h, est_h,
    est, state, noise, modulation, frames, blocks, w_in, w_out, queries, kv, bias, mixed, mixed_sib,
    own_sum, far_sum, far_in, next_out, next_in, passing, moved, moved_in, pace,
    store_sem, load_sem, send_sem, recv_sem, pair_send, pair_recv,
    far_send, far_recv, next_send, next_recv, extra_send, move_send, move_recv, pace_send, pace_recv, pass_send, pass_recv,
):
    width = state.shape[1]
    inner = w_out.shape[1]
    chunks, _, span = own_sum.shape
    slot = lax.axis_index("queue")
    shard = lax.axis_index("shard")
    side = lax.div(shard, 2)
    core = lax.rem(shard, 2)
    other = 1 - core
    last = 2 * lax.axis_size("queue") - 1
    chip = 2 * slot + side

    def at(step, which):
        there = chip + step
        return (lax.div(there, 2), 2 * lax.rem(there, 2) + which)

    sibling = (slot, 2 * side + other)
    turn = lax.rem(chip, 4)
    detour = (turn == 3) & (chip <= last - 3)
    relays = (turn == 2) & (chip <= last - 4)
    has_behind = chip > 0
    has_ahead = chip < last
    low_extra = chip == 1
    high_extra = chip == last - 1

    barrier = pltpu.get_barrier_semaphore()

    def greet(condition, device):
        @pl.when(condition)
        def _():
            pl.semaphore_signal(barrier, inc=1, device_id=device, device_id_type=MESH)

    pl.semaphore_signal(barrier, inc=1, device_id=sibling, device_id_type=MESH)
    greet(has_behind, at(-1, core))
    greet(has_ahead, at(1, core))
    greet((core == 0) & has_behind, at(-1, 1))
    greet((core == 0) & (chip == 0), at(1, 1))
    for k in range(2):
        greet((core == 0) & (chip >= 3), at(jnp.where(turn == 2, -4, -3), k))
    greet((core == 1) & has_ahead, at(1, 0))
    greet((core == 1) & has_behind, at(-1, 0))

    def count(condition):
        return jnp.where(condition, 1, 0)

    greeted = (
        1 + count(has_ahead) + count(has_behind)
        + count((core == 0) & has_behind) + count((core == 0) & has_ahead)
        + count((core == 1) & has_ahead) + count((core == 1) & low_extra)
        + count((chip <= last - 3) & (turn != 3)) + count(relays)
    )

    def load(source, target, n):
        copy = pltpu.make_async_copy(source, target, load_sem.at[n])
        copy.start()
        return copy

    load_state = [
        load(state_h.at[pl.ds(k * HALF, HALF)], state.at[pl.ds(k * HALF, HALF)], k) for k in range(2)
    ]
    load_mod = load(mod_h, modulation, 2)
    load_frames = load(frame_h, frames, 3)

    level = step_ref[0]
    sigma_now = plan_ref[level]
    sigma_step = plan_ref[level + 1] - sigma_now
    load_mod.wait()
    modulate = modulation[level].astype(F32)
    shift, gain, gate = modulate[0:1], 1.0 + modulate[1:2], modulate[2:3]
    def send(place, half, to_place, device, n):
        rows = pl.ds(half * HALF, HALF)
        return pltpu.make_async_remote_copy(
            src_ref=blocks.at[place, rows],
            dst_ref=blocks.at[to_place, rows],
            send_sem=send_sem.at[n],
            recv_sem=recv_sem.at[to_place, half],
            device_id=device,
            device_id_type=MESH,
        )

    def wait_block(place, half):
        here = blocks.at[place, pl.ds(half * HALF, HALF)]
        pltpu.make_async_copy(here, here, recv_sem.at[place, half]).wait()

    to_ahead = [send(4 + core, half, 2 + core, at(1, core), half) for half in range(2)]
    to_behind = [send(4 + core, half, 6 + core, at(-1, core), 2 + half) for half in range(2)]
    to_sibling = [send(4 + core, half, 4 + core, sibling, 4 + half) for half in range(2)]
    for half in range(2):
        load_state[half].wait()
        for n in range(3 * half, 3 * half + 3):
            rows = pl.ds(n * 16, 16)
            x = state[rows, :]
            x = x - jnp.mean(x, axis=-1, keepdims=True)
            spread = jnp.mean(jnp.square(x), axis=-1, keepdims=True)
            blocks[4 + core, rows, :] = (x * lax.rsqrt(spread + 1e-06) * gain + shift).astype(BF16)
        if half == 0:
            pl.semaphore_wait(barrier, greeted)
        pl.when(has_ahead)(to_ahead[half].start)
        pl.when(has_behind)(to_behind[half].start)
        to_sibling[half].start()
    load_w = [
        load(w, w_in.at[:, pl.ds(n * inner, inner)], 4 + n)
        for n, w in enumerate((wq_h, wk_h, wv_h))
    ]

    pace[0] = sigma_step * gate
    step = 2 * core - 1
    paces = [
        pltpu.make_async_remote_copy(
            src_ref=pace.at[0], dst_ref=pace.at[2 - core],
            send_sem=pace_send.at[k], recv_sem=pace_recv.at[1 - core],
            device_id=at(step, k), device_id_type=MESH,
        )
        for k in range(2)
    ]
    gives = chip <= last - 2
    gives_pace = gives & ((core == 1) | has_behind)
    for copy in paces:
        pl.when(gives_pace)(copy.start)

    load_frames.wait()
    lines_all = (last + 1) * 192 // 128
    first = 192 * chip - 288 + (last + 1) * 192
    row = lax.div(first, 128)
    line = jnp.concatenate(
        [frames[pl.ds(lax.rem(row + n, lines_all), 1), :] for n in range(7)], axis=1
    ).astype(F32)
    line = jnp.broadcast_to(line, (8, 896))
    line = jnp.where(side == 0, pltpu.roll(line, 896 - 96, 1), pltpu.roll(line, 896 - 32, 1))
    column = jnp.broadcast_to(pltpu.roll(line, 896 - 96, 1)[0:1, :640], (128, 640)).T
    for n in range(4):
        keys = line if n == 0 else pltpu.roll(line, 896 - 96 * n, 1)
        gap = jnp.abs(column[(n + 1) * ROWS:(n + 2) * ROWS, 0:1] - keys[0:1, :512])
        bias[n] = jnp.where(gap <= 1.0, 0.0, -1e30)
    for condition, n, start in ((low_extra, 0, 0), (high_extra, 5, 3)):
        @pl.when(condition)
        def _():
            keys = line if start == 0 else pltpu.roll(line, 896 - 96 * start, 1)
            gap = jnp.abs(column[n * ROWS:(n + 1) * ROWS, 0:1] - keys[0:1, :512])
            bias[4] = jnp.where(gap <= 1.0, 0.0, -1e30)
    kv[pl.ds(8 * ROWS, 32), :] = jnp.zeros((32, 2 * inner), BF16)
    for condition, place in (
        (chip < 2, 1), (chip == 0, 2), (chip == 0, 3),
        (chip == last, 6), (chip == last, 7), (chip > last - 2, 0),
    ):
        @pl.when(condition)
        def _():
            blocks[place] = jnp.zeros((ROWS, width), BF16)

    def gather(parts):
        return jnp.concatenate([blocks[p, r:r + k] for p, r, k in parts], axis=0)

    def project_q(parts, into):
        for n in range(inner // 256):
            y = jnp.dot(gather(parts), w_in[:, n * 256:(n + 1) * 256], preferred_element_type=F32)
            y = y.astype(BF16) * 0.125
            done = 0
            for (_, _, k), r in zip(parts, into):
                queries[r:r + k, n * 256:(n + 1) * 256] = y[done:done + k]
                done += k

    def project_kv(parts, into):
        def part(n, _):
            cols = pl.ds(pl.multiple_of(n * 256, 256), 256)
            w = w_in[:, pl.ds(pl.multiple_of(inner + n * 256, 256), 256)]
            y = jnp.dot(gather(parts), w, preferred_element_type=F32).astype(BF16)
            done = 0
            for (_, _, k), r in zip(parts, into):
                kv[r:r + k, cols] = y[done:done + k]
                done += k
            return 0
        lax.fori_loop(0, 2 * inner // 256, part, 0)

    low = lax.broadcasted_iota(jnp.int32, (ROWS, 128), 1) < 64

    def attend(n, start):
        for g in range(inner // 128):
            q = queries[n * ROWS:(n + 1) * ROWS, g * 128:(g + 1) * 128]
            zero = jnp.zeros_like(q)
            q = jnp.concatenate([jnp.where(low, q, zero), jnp.where(low, zero, q)], axis=0)
            k = kv[start * ROWS:start * ROWS + 512, g * 128:(g + 1) * 128]
            v = kv[start * ROWS:start * ROWS + 512, inner + g * 128:inner + (g + 1) * 128]
            s = lax.dot_general(q, k, (((1,), (1,)), ((), ())), preferred_element_type=F32)
            s = s + jnp.concatenate([bias[n], bias[n]], axis=0)
            w = jnp.exp(s - jnp.max(s, axis=-1, keepdims=True))
            total = jnp.sum(w, axis=-1, keepdims=True)
            o = jnp.dot(w.astype(BF16), v, preferred_element_type=F32) / total
            mixed[n, :, g * 128:(g + 1) * 128] = jnp.where(low, o[:ROWS], o[ROWS:]).astype(BF16)

    for half in range(2):
        wait_block(4 + other, half)
    for copy in load_w:
        copy.wait()
    load_wo = load(wo_h, w_out.at[0], 7)
    load_noise = load(noise_h, noise, 8)
    share_w = pltpu.make_async_remote_copy(
        src_ref=wo_h, dst_ref=w_out.at[1], send_sem=pair_send.at[0], recv_sem=pair_recv.at[0],
        device_id=sibling, device_id_type=MESH,
    )
    share_w.start()
    project_q([(4, 0, 96), (5, 0, 96)], (ROWS, 2 * ROWS))
    project_kv([(4, 0, 96), (5, 0, 96)], (3 * ROWS, 4 * ROWS))

    core_rows = pl.ds(pl.multiple_of(core * HALF, 16), HALF)
    other_rows = pl.ds(pl.multiple_of(other * HALF, 16), HALF)
    both = has_behind & has_ahead

    def forward(place, half, n):
        wait_block(place, half)
        send(place, half, place, sibling, n).start()

    def relay(place, to_place, device, n):
        return pltpu.make_async_remote_copy(
            src_ref=blocks.at[place, core_rows], dst_ref=blocks.at[to_place, core_rows],
            send_sem=send_sem.at[n], recv_sem=recv_sem.at[to_place, core],
            device_id=device, device_id_type=MESH,
        )

    relay_ahead = relay(3, 1, at(1, core), 10)
    relay_behind = relay(6, 0, at(-1, core), 11)

    def when(condition, *steps):
        @pl.when(condition)
        def _():
            for step in steps:
                step()

    def neighbours(half):
        first_core, second_core = core == 0, core == 1
        when(first_core & has_behind, lambda: forward(2, half, 6 + half))
        when(first_core & has_ahead, lambda: forward(6, half, 8 + half))
        when(second_core & has_behind, lambda: forward(3, half, 6 + half))
        if half == 1:
            when(second_core & both, relay_ahead.start)
        else:
            when(first_core & both, relay_behind.start)
        when(second_core & has_ahead, lambda: forward(7, half, 8 + half))
        when(first_core & has_behind, lambda: wait_block(3, half))
        if half == 0:
            when(first_core & both, relay_ahead.start)
        when(first_core & has_ahead, lambda: wait_block(7, half))
        when(second_core & has_ahead, lambda: wait_block(6, half))
        if half == 1:
            when(second_core & both, relay_behind.start)
        when(second_core & has_behind, lambda: wait_block(2, half))
        r = half * HALF
        project_q([(3, r, HALF), (6, r, HALF)], (r, 3 * ROWS + r))
        project_kv(
            [(2, r, HALF), (3, r, HALF), (6, r, HALF), (7, r, HALF)],
            (ROWS + r, 2 * ROWS + r, 5 * ROWS + r, 6 * ROWS + r),
        )

    neighbours(0)
    neighbours(1)
    attend(1, 1)
    attend(2, 2)

    def swap(source, start, rows, n):
        return pltpu.make_async_remote_copy(
            src_ref=source, dst_ref=mixed_sib.at[pl.ds(start, rows)],
            send_sem=pair_send.at[n], recv_sem=pair_recv.at[n],
            device_id=sibling, device_id_type=MESH,
        )

    swap_own = swap(mixed.at[1 + other], ROWS, ROWS, 1)
    swap_own.start()

    def forward_far(k):
        here = blocks.at[k, core_rows]
        pltpu.make_async_copy(here, here, recv_sem.at[k, core]).wait()
        pltpu.make_async_remote_copy(
            src_ref=here, dst_ref=here, send_sem=send_sem.at[12 + k],
            recv_sem=recv_sem.at[k, core], device_id=sibling, device_id_type=MESH,
        ).start()

    def wait_far(k):
        here = blocks.at[k, other_rows]
        pltpu.make_async_copy(here, here, recv_sem.at[k, other]).wait()

    when(chip >= 2, lambda: forward_far(1))
    when(chip <= last - 2, lambda: forward_far(0))

    load_wo.wait()
    share_w.wait()
    swap_own.wait()
    moves = []
    low_end = (chip == 0) & (core == 0)
    which = jnp.where(low_end, 2, 1 - core)
    place = pl.multiple_of(which * HALF, 16)
    for n in range(chunks):
        cols = slice(n * span, (n + 1) * span)
        y = jnp.dot(mixed[1 + core], w_out[0, :, cols], preferred_element_type=F32)
        y += jnp.dot(mixed_sib[ROWS:2 * ROWS], w_out[1, :, cols], preferred_element_type=F32)
        own_sum[n] = y
        moved[n] = (state[:, cols] + pace[0, :, cols] * y).astype(BF16)
        for k in range(2):
            copy = pltpu.make_async_remote_copy(
                src_ref=moved.at[n, pl.ds(k * HALF, HALF)], dst_ref=moved_in.at[n, pl.ds(place, HALF)],
                send_sem=move_send.at[n, k],
                recv_sem=move_recv.at[n, which],
                device_id=at(jnp.where(low_end, 1, step), k), device_id_type=MESH,
            )
            pl.when(gives)(copy.start)
            moves.append(copy)

    def wait_moved(condition, n, k):
        here = moved_in.at[n, pl.ds(k * HALF, HALF)]
        when(condition, lambda: pltpu.make_async_copy(here, here, move_recv.at[n, k]).wait())

    def project_out(mine, theirs, n):
        cols = slice(n * span, (n + 1) * span)
        y = jnp.dot(mine, w_out[0, :, cols], preferred_element_type=F32)
        y += jnp.dot(theirs, w_out[1, :, cols], preferred_element_type=F32)
        return y

    def give(source, target, n, half, device, send, recv):
        return pltpu.make_async_remote_copy(
            src_ref=source, dst_ref=target.at[n, core_rows],
            send_sem=send, recv_sem=recv.at[n, core],
            device_id=device, device_id_type=MESH,
        )

    swap_extra = swap(mixed.at[4, other_rows], 2 * ROWS, HALF, 5)
    third = pl.ds(ROWS, HALF)

    def extra(n, device):
        return give(far_sum.at[n, third], far_in, n, 2, device, extra_send.at[n, 0], far_recv)

    def extra_next(n):
        return give(next_out.at[n, third], next_in, n, 2, at(1, 0), extra_send.at[n, 1], next_recv)

    when(low_extra, lambda: project_q([(2, 0, ROWS)], (4 * ROWS,)), lambda: attend(4, 0))
    when(high_extra, lambda: project_q([(7, 0, ROWS)], (4 * ROWS,)), lambda: attend(4, 3))

    when(low_extra | high_extra, swap_extra.start)
    when(chip >= 2, lambda: wait_far(1))
    when(chip <= last - 2, lambda: wait_far(0))
    project_kv([(0, 0, ROWS), (1, 0, ROWS)], (7 * ROWS, 0))
    attend(0, 0)
    swap_low = swap(mixed.at[0, other_rows], 0, HALF, 2)
    swap_low.start()
    attend(3, 3)
    swap_high = swap(mixed.at[3, other_rows], HALF, HALF, 3)
    swap_high.start()
    swap_low.wait()
    swap_high.wait()

    for condition, k in ((both, 0), (chip <= last - 3, 1)):
        here = pace.at[1 + k]
        when(condition, pltpu.make_async_copy(here, here, pace_recv.at[k]).wait)
    far = []
    far_mine = jnp.concatenate([mixed[0, core_rows, :], mixed[3, core_rows, :]], axis=0)
    for n in range(chunks):
        cols = slice(n * span, (n + 1) * span)
        y = project_out(far_mine, mixed_sib[0:ROWS], n)
        far_sum[n, 0:ROWS] = y.astype(BF16)
        wait_moved(both, n, 0)
        wait_moved(chip <= last - 3, n, 1)
        for k in range(2):
            rows = pl.ds(k * HALF, HALF)
            base = moved_in[n, rows].astype(F32)
            next_out[n, rows] = (base + pace[1 + k, :, cols] * y[k * HALF:(k + 1) * HALF]).astype(BF16)
        below, above = far_sum.at[n, pl.ds(0, HALF)], far_sum.at[n, pl.ds(HALF, HALF)]
        next_below, next_above = next_out.at[n, pl.ds(0, HALF)], next_out.at[n, pl.ds(HALF, HALF)]
        group = (
            (has_behind, give(below, far_in, n, 0, at(-1, 1), far_send.at[n, 0], far_recv)),
            (has_ahead, give(above, far_in, n, 1, at(1, 0), far_send.at[n, 1], far_recv)),
            (both, give(next_below, next_in, n, 0, at(1, 1), next_send.at[n, 0], next_recv)),
            ((chip <= last - 3) & (turn != 3), give(next_above, next_in, n, 1, at(3, 0), next_send.at[n, 1], next_recv)),
            (detour, pltpu.make_async_remote_copy(
                src_ref=next_above, dst_ref=passing.at[n], send_sem=next_send.at[n, 1],
                recv_sem=pass_recv.at[n], device_id=at(-1, core), device_id_type=MESH,
            )),
        )
        for condition, copy in group[:0:-1]:
            pl.when(condition)(copy.start)
        far.extend(group)
    for n in range(chunks):
        condition, copy = far[5 * n]
        pl.when(condition)(copy.start)

    @pl.when(low_extra | high_extra)
    def _():
        swap_extra.wait()
        for n in range(chunks):
            cols = slice(n * span, (n + 1) * span)
            y = project_out(mixed[4, core_rows], mixed_sib[2 * ROWS:2 * ROWS + HALF], n)
            far_sum[n, third] = y.astype(BF16)
            wait_moved(low_extra, n, 2)
            base = moved_in[n, third].astype(F32)
            next_out[n, third] = (base + pace[0, :, cols] * y).astype(BF16)
            when(low_extra, extra(n, at(-1, 0)).start, extra_next(n).start)
            when(high_extra, extra(n, at(1, 1)).start)

    def wait_halves(target, n, sem):
        for k in range(2):
            here = target.at[n, pl.ds(k * HALF, HALF)]
            pltpu.make_async_copy(here, here, sem.at[n, k]).wait()

    def onward(n):
        return give(passing.at[n], next_in, n, 1, at(4, 0), pass_send.at[n], next_recv)

    def pass_on(n):
        pltpu.make_async_copy(passing.at[n], passing.at[n], pass_recv.at[n]).wait()
        onward(n).start()

    when(relays, *[functools.partial(pass_on, n) for n in range(chunks)])
    load_noise.wait()

    def store(source, target, n):
        return pltpu.make_async_copy(source, target, store_sem.at[n])

    when(slot == 0, store(noise, adv_h, 0).start)
    stores = []
    for n in range(chunks):
        cols = slice(n * span, (n + 1) * span)
        wait_halves(far_in, n, far_recv)
        velocity = gate[:, cols] * (own_sum[n] + far_in[n].astype(F32))
        est[:, cols] = (state[:, cols] - sigma_now * velocity).astype(BF16)

        @pl.when(slot > 0)
        def _():
            wait_halves(next_in, n, next_recv)
            store(next_in.at[n], adv_h.at[:, pl.ds(n * span, span)], 1 + n).start()

        here = pl.ds(n * span, span)
        stores.append(store(est.at[:, here], est_h.at[:, here], 1 + chunks + n))
        stores[-1].start()

    for n in range(chunks):
        when(slot > 0, store(next_in.at[n], adv_h.at[:, pl.ds(n * span, span)], 1 + n).wait)
    when(slot == 0, store(noise, adv_h, 0).wait)
    for copy in stores:
        copy.wait()

    def left(condition, n):
        here = blocks.at[0, pl.ds(0, HALF)]
        when(condition, lambda: pltpu.make_async_copy(here, here, send_sem.at[n]).wait())

    for half in range(2):
        left(has_ahead, half)
        left(has_behind, 2 + half)
        left(chip >= 0, 4 + half)
        left(has_behind, 6 + half)
        left(has_ahead, 8 + half)
    left(both, 10)
    left(both, 11)
    left(chip <= last - 2, 12)
    left(chip >= 2, 13)
    for condition, copy in far:
        when(condition, copy.wait_send)
    for n in range(chunks):
        when(relays, onward(n).wait_send)
    when(gives_pace, *[copy.wait_send for copy in paces])
    when(gives, *[copy.wait_send for copy in moves])
    for n in range(chunks):
        when(low_extra, extra(n, at(-1, 0)).wait_send, extra_next(n).wait_send)
        when(high_extra, extra(n, at(1, 1)).wait_send)


def finish(adv_in, est_in, adv_out, est_out, adv_bf16, adv, est, sem):
    size = ROWS // 2
    rows = [pl.ds(k * size, size) for k in range(2)]
    ins = [pltpu.make_async_copy(adv_in.at[r], adv_bf16.at[r], sem.at[k]) for k, r in enumerate(rows)]
    ins.append(pltpu.make_async_copy(est_in, est, sem.at[2]))
    outs = [pltpu.make_async_copy(adv.at[r], adv_out.at[r], sem.at[3 + k]) for k, r in enumerate(rows)]
    outs.append(pltpu.make_async_copy(est, est_out, sem.at[5]))
    for copy in ins:
        copy.start()
    for k, r in enumerate(rows):
        ins[k].wait()
        adv[r, :] = adv_bf16[r, :].astype(F32)
        outs[k].start()
    ins[2].wait()
    outs[2].start()
    for copy in outs:
        copy.wait()


def on_device(state, noise, modulation, timesteps, plan, frame_ids, w_query, w_key, w_value, w_out):
    rows, width = state.shape
    inner = w_query.shape[1]
    span = 512
    chunks = width // span
    hbm = pl.BlockSpec(memory_space=pltpu.HBM)
    smem = pl.BlockSpec(memory_space=pltpu.SMEM)
    dma = pltpu.SemaphoreType.DMA
    advanced, estimate = pl.pallas_call(
        kernel,
        out_shape=(
            jax.ShapeDtypeStruct((rows, width), BF16),
            jax.ShapeDtypeStruct((rows, width), BF16),
        ),
        in_specs=[hbm, hbm, hbm, smem, smem, hbm, hbm, hbm, hbm, hbm],
        out_specs=(hbm, hbm),
        scratch_shapes=[
            pltpu.VMEM((rows, width), BF16),
            pltpu.VMEM((rows, width), F32),
            pltpu.VMEM((rows, width), BF16),
            pltpu.VMEM(modulation.shape, BF16),
            pltpu.VMEM((frame_ids.size // 128, 128), jnp.int32),
            pltpu.VMEM((8, rows, width), BF16),
            pltpu.VMEM((width, 3 * inner), BF16),
            pltpu.VMEM((2, inner, width), BF16),
            pltpu.VMEM((5 * rows, inner), BF16),
            pltpu.VMEM((8 * rows + 32, 2 * inner), BF16),
            pltpu.VMEM((5, rows, 512), F32),
            pltpu.VMEM((5, rows, inner), BF16),
            pltpu.VMEM((3 * rows, inner), BF16),
            pltpu.VMEM((chunks, rows, span), F32),
            pltpu.VMEM((chunks, rows + HALF, span), BF16),
            pltpu.VMEM((chunks, rows, span), BF16),
            pltpu.VMEM((chunks, rows + HALF, span), BF16),
            pltpu.VMEM((chunks, rows, span), BF16),
            pltpu.VMEM((chunks, HALF, span), BF16),
            pltpu.VMEM((chunks, rows, span), BF16),
            pltpu.VMEM((chunks, rows + HALF, span), BF16),
            pltpu.VMEM((3, 1, width), F32),
            dma((1 + 2 * chunks,)),
            dma((9,)),
            dma((14,)),
            dma((8, 2)),
            dma((6,)),
            dma((6,)),
            dma((chunks, 2)),
            dma((chunks, 2)),
            dma((chunks, 2)),
            dma((chunks, 2)),
            dma((chunks, 2)),
            dma((chunks, 2)),
            dma((chunks, 3)),
            dma((2,)),
            dma((2,)),
            dma((chunks,)),
            dma((chunks,)),
        ],
        compiler_params=pltpu.CompilerParams(
            collective_id=0, has_side_effects=True, vmem_limit_bytes=62914560
        ),
        name="step",
    )(
        state, noise, modulation, timesteps, plan, frame_ids.reshape(-1, 128),
        w_query, w_key, w_value, w_out,
    )
    return pl.pallas_call(
        finish,
        out_shape=(
            jax.ShapeDtypeStruct((rows, width), F32),
            jax.ShapeDtypeStruct((rows, width), BF16),
        ),
        in_specs=[hbm, hbm],
        out_specs=(hbm, hbm),
        scratch_shapes=[
            pltpu.VMEM((rows, width), BF16),
            pltpu.VMEM((rows, width), F32),
            pltpu.VMEM((rows, width), BF16),
            dma((6,)),
        ],
        name="finish",
    )(advanced, estimate)


def solution(mesh):
    return jax.shard_map(
        on_device,
        mesh=mesh,
        in_specs=(
            P(("queue", "shard"), None),
            P("shard", None),
            P(),
            P("queue"),
            P(),
            P(),
            P(None, "shard"),
            P(None, "shard"),
            P(None, "shard"),
            P("shard", None),
        ),
        out_specs=(P(("queue", "shard"), None), P(("queue", "shard"), None)),
        check_vma=False,
    )
```

```python
import functools

import jax
import jax.numpy as jnp
from jax import lax
from jax.experimental import pallas as pl
from jax.experimental.pallas import tpu as pltpu
from jax.sharding import PartitionSpec as P

MESH = pl.DeviceIdType.MESH
ROWS = 96
HALF = 48
BF16 = jnp.bfloat16
F32 = jnp.float32


def kernel(
    state_h, noise_h, mod_h, step_ref, plan_ref, frame_h, wq_h, wk_h, wv_h, wo_h,
    adv_h, est_h,
    est, state, noise, modulation, frames, blocks, w_in, w_out, queries, kv, bias, mixed, mixed_sib,
    own_sum, far_sum, far_in, next_out, next_in, passing, moved, moved_in, pace,
    store_sem, load_sem, send_sem, recv_sem, pair_send, pair_recv,
    far_send, far_recv, next_send, next_recv, extra_send, move_send, move_recv, pace_send, pace_recv, pass_send, pass_recv,
):
    width = state.shape[1]
    inner = w_out.shape[1]
    chunks, _, span = own_sum.shape
    slot = lax.axis_index("queue")
    shard = lax.axis_index("shard")
    side = lax.div(shard, 2)
    core = lax.rem(shard, 2)
    other = 1 - core
    last = 2 * lax.axis_size("queue") - 1
    chip = 2 * slot + side

    def at(step, which):
        there = chip + step
        return (lax.div(there, 2), 2 * lax.rem(there, 2) + which)

    sibling = (slot, 2 * side + other)
    turn = lax.rem(chip, 4)
    detour = (turn == 3) & (chip <= last - 3)
    relays = (turn == 2) & (chip <= last - 4)
    has_behind = chip > 0
    has_ahead = chip < last
    low_extra = chip == 1
    high_extra = chip == last - 1

    barrier = pltpu.get_barrier_semaphore()

    def greet(condition, device):
        @pl.when(condition)
        def _():
            pl.semaphore_signal(barrier, inc=1, device_id=device, device_id_type=MESH)

    pl.semaphore_signal(barrier, inc=1, device_id=sibling, device_id_type=MESH)
    greet(has_behind, at(-1, core))
    greet(has_ahead, at(1, core))
    greet((core == 0) & has_behind, at(-1, 1))
    greet((core == 0) & (chip == 0), at(1, 1))
    for k in range(2):
        greet((core == 0) & (chip >= 3), at(jnp.where(turn == 2, -4, -3), k))
    greet((core == 1) & has_ahead, at(1, 0))
    greet((core == 1) & has_behind, at(-1, 0))

    def count(condition):
        return jnp.where(condition, 1, 0)

    greeted = (
        1 + count(has_ahead) + count(has_behind)
        + count((core == 0) & has_behind) + count((core == 0) & has_ahead)
        + count((core == 1) & has_ahead) + count((core == 1) & low_extra)
        + count((chip <= last - 3) & (turn != 3)) + count(relays)
    )

    def load(source, target, n):
        copy = pltpu.make_async_copy(source, target, load_sem.at[n])
        copy.start()
        return copy

    load_state = [
        load(state_h.at[pl.ds(k * HALF, HALF)], state.at[pl.ds(k * HALF, HALF)], k) for k in range(2)
    ]
    load_mod = load(mod_h, modulation, 2)
    load_frames = load(frame_h, frames, 3)

    level = step_ref[0]
    sigma_now = plan_ref[level]
    sigma_step = plan_ref[level + 1] - sigma_now
    load_mod.wait()
    modulate = modulation[level].astype(F32)
    shift, gain, gate = modulate[0:1], 1.0 + modulate[1:2], modulate[2:3]
    def send(place, half, to_place, device, n):
        rows = pl.ds(half * HALF, HALF)
        return pltpu.make_async_remote_copy(
            src_ref=blocks.at[place, rows],
            dst_ref=blocks.at[to_place, rows],
            send_sem=send_sem.at[n],
            recv_sem=recv_sem.at[to_place, half],
            device_id=device,
            device_id_type=MESH,
        )

    def wait_block(place, half):
        here = blocks.at[place, pl.ds(half * HALF, HALF)]
        pltpu.make_async_copy(here, here, recv_sem.at[place, half]).wait()

    to_ahead = [send(4 + core, half, 2 + core, at(1, core), half) for half in range(2)]
    to_behind = [send(4 + core, half, 6 + core, at(-1, core), 2 + half) for half in range(2)]
    to_sibling = [send(4 + core, half, 4 + core, sibling, 4 + half) for half in range(2)]
    for half in range(2):
        load_state[half].wait()
        for n in range(3 * half, 3 * half + 3):
            rows = pl.ds(n * 16, 16)
            x = state[rows, :]
            x = x - jnp.mean(x, axis=-1, keepdims=True)
            spread = jnp.mean(jnp.square(x), axis=-1, keepdims=True)
            blocks[4 + core, rows, :] = (x * lax.rsqrt(spread + 1e-06) * gain + shift).astype(BF16)
        if half == 0:
            pl.semaphore_wait(barrier, greeted)
        pl.when(has_ahead)(to_ahead[half].start)
        pl.when(has_behind)(to_behind[half].start)
        to_sibling[half].start()
    load_w = [
        load(w, w_in.at[:, pl.ds(n * inner, inner)], 4 + n)
        for n, w in enumerate((wq_h, wk_h, wv_h))
    ]

    pace[0] = sigma_step * gate
    step = 2 * core - 1
    paces = [
        pltpu.make_async_remote_copy(
            src_ref=pace.at[0], dst_ref=pace.at[2 - core],
            send_sem=pace_send.at[k], recv_sem=pace_recv.at[1 - core],
            device_id=at(step, k), device_id_type=MESH,
        )
        for k in range(2)
    ]
    gives = chip <= last - 2
    gives_pace = gives & ((core == 1) | has_behind)
    for copy in paces:
        pl.when(gives_pace)(copy.start)

    load_frames.wait()
    lines_all = (last + 1) * 192 // 128
    first = 192 * chip - 288 + (last + 1) * 192
    row = lax.div(first, 128)
    line = jnp.concatenate(
        [frames[pl.ds(lax.rem(row + n, lines_all), 1), :] for n in range(7)], axis=1
    ).astype(F32)
    line = jnp.broadcast_to(line, (8, 896))
    line = jnp.where(side == 0, pltpu.roll(line, 896 - 96, 1), pltpu.roll(line, 896 - 32, 1))
    column = jnp.broadcast_to(pltpu.roll(line, 896 - 96, 1)[0:1, :640], (128, 640)).T
    for n in range(4):
        keys = line if n == 0 else pltpu.roll(line, 896 - 96 * n, 1)
        gap = jnp.abs(column[(n + 1) * ROWS:(n + 2) * ROWS, 0:1] - keys[0:1, :512])
        bias[n] = jnp.where(gap <= 1.0, 0.0, -1e30)
    for condition, n, start in ((low_extra, 0, 0), (high_extra, 5, 3)):
        @pl.when(condition)
        def _():
            keys = line if start == 0 else pltpu.roll(line, 896 - 96 * start, 1)
            gap = jnp.abs(column[n * ROWS:(n + 1) * ROWS, 0:1] - keys[0:1, :512])
            bias[4] = jnp.where(gap <= 1.0, 0.0, -1e30)
    kv[pl.ds(8 * ROWS, 32), :] = jnp.zeros((32, 2 * inner), BF16)
    for condition, place in (
        (chip < 2, 1), (chip == 0, 2), (chip == 0, 3),
        (chip == last, 6), (chip == last, 7), (chip > last - 2, 0),
    ):
        @pl.when(condition)
        def _():
            blocks[place] = jnp.zeros((ROWS, width), BF16)

    def gather(parts):
        return jnp.concatenate([blocks[p, r:r + k] for p, r, k in parts], axis=0)

    def project_q(parts, into):
        for n in range(inner // 256):
            y = jnp.dot(gather(parts), w_in[:, n * 256:(n + 1) * 256], preferred_element_type=F32)
            y = y.astype(BF16) * 0.125
            done = 0
            for (_, _, k), r in zip(parts, into):
                queries[r:r + k, n * 256:(n + 1) * 256] = y[done:done + k]
                done += k

    def project_kv(parts, into):
        def part(n, _):
            cols = pl.ds(pl.multiple_of(n * 256, 256), 256)
            w = w_in[:, pl.ds(pl.multiple_of(inner + n * 256, 256), 256)]
            y = jnp.dot(gather(parts), w, preferred_element_type=F32).astype(BF16)
            done = 0
            for (_, _, k), r in zip(parts, into):
                kv[r:r + k, cols] = y[done:done + k]
                done += k
            return 0
        lax.fori_loop(0, 2 * inner // 256, part, 0)

    low = lax.broadcasted_iota(jnp.int32, (ROWS, 128), 1) < 64

    def attend(n, start):
        for g in range(inner // 128):
            q = queries[n * ROWS:(n + 1) * ROWS, g * 128:(g + 1) * 128]
            zero = jnp.zeros_like(q)
            q = jnp.concatenate([jnp.where(low, q, zero), jnp.where(low, zero, q)], axis=0)
            k = kv[start * ROWS:start * ROWS + 512, g * 128:(g + 1) * 128]
            v = kv[start * ROWS:start * ROWS + 512, inner + g * 128:inner + (g + 1) * 128]
            s = lax.dot_general(q, k, (((1,), (1,)), ((), ())), preferred_element_type=F32)
            s = s + jnp.concatenate([bias[n], bias[n]], axis=0)
            w = jnp.exp(s - jnp.max(s, axis=-1, keepdims=True))
            total = jnp.sum(w, axis=-1, keepdims=True)
            o = jnp.dot(w.astype(BF16), v, preferred_element_type=F32) / total
            mixed[n, :, g * 128:(g + 1) * 128] = jnp.where(low, o[:ROWS], o[ROWS:]).astype(BF16)

    for half in range(2):
        wait_block(4 + other, half)
    for copy in load_w:
        copy.wait()
    load_wo = load(wo_h, w_out.at[0], 7)
    load_noise = load(noise_h, noise, 8)
    share_w = pltpu.make_async_remote_copy(
        src_ref=wo_h, dst_ref=w_out.at[1], send_sem=pair_send.at[0], recv_sem=pair_recv.at[0],
        device_id=sibling, device_id_type=MESH,
    )
    share_w.start()
    project_q([(4, 0, 96), (5, 0, 96)], (ROWS, 2 * ROWS))
    project_kv([(4, 0, 96), (5, 0, 96)], (3 * ROWS, 4 * ROWS))

    core_rows = pl.ds(pl.multiple_of(core * HALF, 16), HALF)
    other_rows = pl.ds(pl.multiple_of(other * HALF, 16), HALF)
    both = has_behind & has_ahead

    def forward(place, half, n):
        wait_block(place, half)
        send(place, half, place, sibling, n).start()

    def relay(place, to_place, device, n):
        return pltpu.make_async_remote_copy(
            src_ref=blocks.at[place, core_rows], dst_ref=blocks.at[to_place, core_rows],
            send_sem=send_sem.at[n], recv_sem=recv_sem.at[to_place, core],
            device_id=device, device_id_type=MESH,
        )

    relay_ahead = relay(3, 1, at(1, core), 10)
    relay_behind = relay(6, 0, at(-1, core), 11)

    def when(condition, *steps):
        @pl.when(condition)
        def _():
            for step in steps:
                step()

    def neighbours(half):
        first_core, second_core = core == 0, core == 1
        when(first_core & has_behind, lambda: forward(2, half, 6 + half))
        when(first_core & has_ahead, lambda: forward(6, half, 8 + half))
        when(second_core & has_behind, lambda: forward(3, half, 6 + half))
        if half == 1:
            when(second_core & both, relay_ahead.start)
        else:
            when(first_core & both, relay_behind.start)
        when(second_core & has_ahead, lambda: forward(7, half, 8 + half))
        when(first_core & has_behind, lambda: wait_block(3, half))
        if half == 0:
            when(first_core & both, relay_ahead.start)
        when(first_core & has_ahead, lambda: wait_block(7, half))
        when(second_core & has_ahead, lambda: wait_block(6, half))
        if half == 1:
            when(second_core & both, relay_behind.start)
        when(second_core & has_behind, lambda: wait_block(2, half))
        r = half * HALF
        project_q([(3, r, HALF), (6, r, HALF)], (r, 3 * ROWS + r))
        project_kv(
            [(2, r, HALF), (3, r, HALF), (6, r, HALF), (7, r, HALF)],
            (ROWS + r, 2 * ROWS + r, 5 * ROWS + r, 6 * ROWS + r),
        )

    neighbours(0)
    neighbours(1)
    attend(1, 1)
    attend(2, 2)

    def swap(source, start, rows, n):
        return pltpu.make_async_remote_copy(
            src_ref=source, dst_ref=mixed_sib.at[pl.ds(start, rows)],
            send_sem=pair_send.at[n], recv_sem=pair_recv.at[n],
            device_id=sibling, device_id_type=MESH,
        )

    swap_own = swap(mixed.at[1 + other], ROWS, ROWS, 1)
    swap_own.start()

    def forward_far(k):
        here = blocks.at[k, core_rows]
        pltpu.make_async_copy(here, here, recv_sem.at[k, core]).wait()
        pltpu.make_async_remote_copy(
            src_ref=here, dst_ref=here, send_sem=send_sem.at[12 + k],
            recv_sem=recv_sem.at[k, core], device_id=sibling, device_id_type=MESH,
        ).start()

    def wait_far(k):
        here = blocks.at[k, other_rows]
        pltpu.make_async_copy(here, here, recv_sem.at[k, other]).wait()

    when(chip >= 2, lambda: forward_far(1))
    when(chip <= last - 2, lambda: forward_far(0))

    load_wo.wait()
    share_w.wait()
    swap_own.wait()
    moves = []
    low_end = (chip == 0) & (core == 0)
    which = jnp.where(low_end, 2, 1 - core)
    place = pl.multiple_of(which * HALF, 16)
    for n in range(chunks):
        cols = slice(n * span, (n + 1) * span)
        y = jnp.dot(mixed[1 + core], w_out[0, :, cols], preferred_element_type=F32)
        y += jnp.dot(mixed_sib[ROWS:2 * ROWS], w_out[1, :, cols], preferred_element_type=F32)
        own_sum[n] = y
        moved[n] = (state[:, cols] + pace[0, :, cols] * y).astype(BF16)
        for k in range(2):
            copy = pltpu.make_async_remote_copy(
                src_ref=moved.at[n, pl.ds(k * HALF, HALF)], dst_ref=moved_in.at[n, pl.ds(place, HALF)],
                send_sem=move_send.at[n, k],
                recv_sem=move_recv.at[n, which],
                device_id=at(jnp.where(low_end, 1, step), k), device_id_type=MESH,
            )
            pl.when(gives)(copy.start)
            moves.append(copy)

    def wait_moved(condition, n, k):
        here = moved_in.at[n, pl.ds(k * HALF, HALF)]
        when(condition, lambda: pltpu.make_async_copy(here, here, move_recv.at[n, k]).wait())

    def project_out(mine, theirs, n):
        cols = slice(n * span, (n + 1) * span)
        y = jnp.dot(mine, w_out[0, :, cols], preferred_element_type=F32)
        y += jnp.dot(theirs, w_out[1, :, cols], preferred_element_type=F32)
        return y

    def give(source, target, n, half, device, send, recv):
        return pltpu.make_async_remote_copy(
            src_ref=source, dst_ref=target.at[n, core_rows],
            send_sem=send, recv_sem=recv.at[n, core],
            device_id=device, device_id_type=MESH,
        )

    swap_extra = swap(mixed.at[4, other_rows], 2 * ROWS, HALF, 5)
    third = pl.ds(ROWS, HALF)

    def extra(n, device):
        return give(far_sum.at[n, third], far_in, n, 2, device, extra_send.at[n, 0], far_recv)

    def extra_next(n):
        return give(next_out.at[n, third], next_in, n, 2, at(1, 0), extra_send.at[n, 1], next_recv)

    when(low_extra, lambda: project_q([(2, 0, ROWS)], (4 * ROWS,)), lambda: attend(4, 0))
    when(high_extra, lambda: project_q([(7, 0, ROWS)], (4 * ROWS,)), lambda: attend(4, 3))

    when(low_extra | high_extra, swap_extra.start)
    when(chip >= 2, lambda: wait_far(1))
    when(chip <= last - 2, lambda: wait_far(0))
    project_kv([(0, 0, ROWS), (1, 0, ROWS)], (7 * ROWS, 0))
    attend(0, 0)
    swap_low = swap(mixed.at[0, other_rows], 0, HALF, 2)
    swap_low.start()
    attend(3, 3)
    swap_high = swap(mixed.at[3, other_rows], HALF, HALF, 3)
    swap_high.start()
    swap_low.wait()
    swap_high.wait()

    for condition, k in ((both, 0), (chip <= last - 3, 1)):
        here = pace.at[1 + k]
        when(condition, pltpu.make_async_copy(here, here, pace_recv.at[k]).wait)
    far = []
    far_mine = jnp.concatenate([mixed[0, core_rows, :], mixed[3, core_rows, :]], axis=0)
    for n in range(chunks):
        cols = slice(n * span, (n + 1) * span)
        y = project_out(far_mine, mixed_sib[0:ROWS], n)
        far_sum[n, 0:ROWS] = y.astype(BF16)
        wait_moved(both, n, 0)
        wait_moved(chip <= last - 3, n, 1)
        for k in range(2):
            rows = pl.ds(k * HALF, HALF)
            base = moved_in[n, rows].astype(F32)
            next_out[n, rows] = (base + pace[1 + k, :, cols] * y[k * HALF:(k + 1) * HALF]).astype(BF16)
        below, above = far_sum.at[n, pl.ds(0, HALF)], far_sum.at[n, pl.ds(HALF, HALF)]
        next_below, next_above = next_out.at[n, pl.ds(0, HALF)], next_out.at[n, pl.ds(HALF, HALF)]
        group = (
            (has_behind, give(below, far_in, n, 0, at(-1, 1), far_send.at[n, 0], far_recv)),
            (has_ahead, give(above, far_in, n, 1, at(1, 0), far_send.at[n, 1], far_recv)),
            (both, give(next_below, next_in, n, 0, at(1, 1), next_send.at[n, 0], next_recv)),
            ((chip <= last - 3) & (turn != 3), give(next_above, next_in, n, 1, at(3, 0), next_send.at[n, 1], next_recv)),
            (detour, pltpu.make_async_remote_copy(
                src_ref=next_above, dst_ref=passing.at[n], send_sem=next_send.at[n, 1],
                recv_sem=pass_recv.at[n], device_id=at(-1, core), device_id_type=MESH,
            )),
        )
        for condition, copy in group[:0:-1]:
            pl.when(condition)(copy.start)
        far.extend(group)
    for n in range(chunks):
        condition, copy = far[5 * n]
        pl.when(condition)(copy.start)

    @pl.when(low_extra | high_extra)
    def _():
        swap_extra.wait()
        for n in range(chunks):
            cols = slice(n * span, (n + 1) * span)
            y = project_out(mixed[4, core_rows], mixed_sib[2 * ROWS:2 * ROWS + HALF], n)
            far_sum[n, third] = y.astype(BF16)
            wait_moved(low_extra, n, 2)
            base = moved_in[n, third].astype(F32)
            next_out[n, third] = (base + pace[0, :, cols] * y).astype(BF16)
            when(low_extra, extra(n, at(-1, 0)).start, extra_next(n).start)
            when(high_extra, extra(n, at(1, 1)).start)

    def wait_halves(target, n, sem):
        for k in range(2):
            here = target.at[n, pl.ds(k * HALF, HALF)]
            pltpu.make_async_copy(here, here, sem.at[n, k]).wait()

    def onward(n):
        return give(passing.at[n], next_in, n, 1, at(4, 0), pass_send.at[n], next_recv)

    def pass_on(n):
        pltpu.make_async_copy(passing.at[n], passing.at[n], pass_recv.at[n]).wait()
        onward(n).start()

    when(relays, *[functools.partial(pass_on, n) for n in range(chunks)])
    load_noise.wait()

    def store(source, target, n):
        return pltpu.make_async_copy(source, target, store_sem.at[n])

    when(slot == 0, store(noise, adv_h, 0).start)
    stores = []
    for n in range(chunks):
        cols = slice(n * span, (n + 1) * span)
        wait_halves(far_in, n, far_recv)
        velocity = gate[:, cols] * (own_sum[n] + far_in[n].astype(F32))
        est[:, cols] = (state[:, cols] - sigma_now * velocity).astype(BF16)

        @pl.when(slot > 0)
        def _():
            wait_halves(next_in, n, next_recv)
            store(next_in.at[n], adv_h.at[:, pl.ds(n * span, span)], 1 + n).start()

        here = pl.ds(n * span, span)
        stores.append(store(est.at[:, here], est_h.at[:, here], 1 + chunks + n))
        stores[-1].start()

    for n in range(chunks):
        when(slot > 0, store(next_in.at[n], adv_h.at[:, pl.ds(n * span, span)], 1 + n).wait)
    when(slot == 0, store(noise, adv_h, 0).wait)
    for copy in stores:
        copy.wait()

    def left(condition, n):
        here = blocks.at[0, pl.ds(0, HALF)]
        when(condition, lambda: pltpu.make_async_copy(here, here, send_sem.at[n]).wait())

    for half in range(2):
        left(has_ahead, half)
        left(has_behind, 2 + half)
        left(chip >= 0, 4 + half)
        left(has_behind, 6 + half)
        left(has_ahead, 8 + half)
    left(both, 10)
    left(both, 11)
    left(chip <= last - 2, 12)
    left(chip >= 2, 13)
    for condition, copy in far:
        when(condition, copy.wait_send)
    for n in range(chunks):
        when(relays, onward(n).wait_send)
    when(gives_pace, *[copy.wait_send for copy in paces])
    when(gives, *[copy.wait_send for copy in moves])
    for n in range(chunks):
        when(low_extra, extra(n, at(-1, 0)).wait_send, extra_next(n).wait_send)
        when(high_extra, extra(n, at(1, 1)).wait_send)


def finish(adv_in, est_in, adv_out, est_out, adv_bf16, adv, est, sem):
    size = ROWS // 3
    rows = [pl.ds(k * size, size) for k in range(3)]
    ins = [pltpu.make_async_copy(adv_in.at[r], adv_bf16.at[r], sem.at[k]) for k, r in enumerate(rows)]
    ins.append(pltpu.make_async_copy(est_in, est, sem.at[3]))
    outs = [pltpu.make_async_copy(adv.at[r], adv_out.at[r], sem.at[4 + k]) for k, r in enumerate(rows)]
    outs.append(pltpu.make_async_copy(est, est_out, sem.at[7]))
    for copy in ins:
        copy.start()
    for k, r in enumerate(rows):
        ins[k].wait()
        adv[r, :] = adv_bf16[r, :].astype(F32)
        outs[k].start()
    ins[3].wait()
    outs[3].start()
    for copy in outs:
        copy.wait()


def on_device(state, noise, modulation, timesteps, plan, frame_ids, w_query, w_key, w_value, w_out):
    rows, width = state.shape
    inner = w_query.shape[1]
    span = 512
    chunks = width // span
    hbm = pl.BlockSpec(memory_space=pltpu.HBM)
    smem = pl.BlockSpec(memory_space=pltpu.SMEM)
    dma = pltpu.SemaphoreType.DMA
    advanced, estimate = pl.pallas_call(
        kernel,
        out_shape=(
            jax.ShapeDtypeStruct((rows, width), BF16),
            jax.ShapeDtypeStruct((rows, width), BF16),
        ),
        in_specs=[hbm, hbm, hbm, smem, smem, hbm, hbm, hbm, hbm, hbm],
        out_specs=(hbm, hbm),
        scratch_shapes=[
            pltpu.VMEM((rows, width), BF16),
            pltpu.VMEM((rows, width), F32),
            pltpu.VMEM((rows, width), BF16),
            pltpu.VMEM(modulation.shape, BF16),
            pltpu.VMEM((frame_ids.size // 128, 128), jnp.int32),
            pltpu.VMEM((8, rows, width), BF16),
            pltpu.VMEM((width, 3 * inner), BF16),
            pltpu.VMEM((2, inner, width), BF16),
            pltpu.VMEM((5 * rows, inner), BF16),
            pltpu.VMEM((8 * rows + 32, 2 * inner), BF16),
            pltpu.VMEM((5, rows, 512), F32),
            pltpu.VMEM((5, rows, inner), BF16),
            pltpu.VMEM((3 * rows, inner), BF16),
            pltpu.VMEM((chunks, rows, span), F32),
            pltpu.VMEM((chunks, rows + HALF, span), BF16),
            pltpu.VMEM((chunks, rows, span), BF16),
            pltpu.VMEM((chunks, rows + HALF, span), BF16),
            pltpu.VMEM((chunks, rows, span), BF16),
            pltpu.VMEM((chunks, HALF, span), BF16),
            pltpu.VMEM((chunks, rows, span), BF16),
            pltpu.VMEM((chunks, rows + HALF, span), BF16),
            pltpu.VMEM((3, 1, width), F32),
            dma((1 + 2 * chunks,)),
            dma((9,)),
            dma((14,)),
            dma((8, 2)),
            dma((6,)),
            dma((6,)),
            dma((chunks, 2)),
            dma((chunks, 2)),
            dma((chunks, 2)),
            dma((chunks, 2)),
            dma((chunks, 2)),
            dma((chunks, 2)),
            dma((chunks, 3)),
            dma((2,)),
            dma((2,)),
            dma((chunks,)),
            dma((chunks,)),
        ],
        compiler_params=pltpu.CompilerParams(
            collective_id=0, has_side_effects=True, vmem_limit_bytes=62914560
        ),
        name="step",
    )(
        state, noise, modulation, timesteps, plan, frame_ids.reshape(-1, 128),
        w_query, w_key, w_value, w_out,
    )
    return pl.pallas_call(
        finish,
        out_shape=(
            jax.ShapeDtypeStruct((rows, width), F32),
            jax.ShapeDtypeStruct((rows, width), BF16),
        ),
        in_specs=[hbm, hbm],
        out_specs=(hbm, hbm),
        scratch_shapes=[
            pltpu.VMEM((rows, width), BF16),
            pltpu.VMEM((rows, width), F32),
            pltpu.VMEM((rows, width), BF16),
            dma((8,)),
        ],
        name="finish",
    )(advanced, estimate)


def solution(mesh):
    return jax.shard_map(
        on_device,
        mesh=mesh,
        in_specs=(
            P(("queue", "shard"), None),
            P("shard", None),
            P(),
            P("queue"),
            P(),
            P(),
            P(None, "shard"),
            P(None, "shard"),
            P(None, "shard"),
            P("shard", None),
        ),
        out_specs=(P(("queue", "shard"), None), P(("queue", "shard"), None)),
        check_vma=False,
    )
```
